256 devices in a mesh: slab: 128 (over y, x_lo, z, core), deg: 2 (over x_hi).
Axes of the slice: x: 4 (x_hi: 2, x_lo: 2; x = x_hi * 2 + x_lo), y: 4, z: 8, core: 2. Of those that a mesh axis runs over, the one named last changes fastest.
Arguments:
- harmonic: bfloat16 [131072, 52, 128], P('slab', 'deg'), may hold values from -6 to 6
- shell: int32 [131072], P('slab'), may hold values from 0 to 63
- atom_type: int32 [131072], P('slab'), may hold values from 0 to 7
- domain: int32 [131072], P('slab'), may hold values from 0 to 1
- form: float32 [8, 256], replicated, may hold values from 0.5 to 4
- bessel: float32 [64, 52, 256], P(None, 'deg'), may hold values from -1 to 1
- wigner: bfloat16 [512, 52, 128, 128], P('slab', 'deg'), may hold values from -0.5 to 0.5
Outputs:
- intensity: float32 [512, 256], P('slab')
The draws below stay inside these ranges and needn't reach their ends.
All inputs are finite; a program needn't handle non-finite values.
Results may differ from the reference program's by a relative error of at most 0.004.
Values may be sent and summed in bfloat16 or wider, within the bound.
No kernel may reach another device: no remote copies, remote signals or barrier semaphores. Data moves between devices by JAX's collectives and lax.ppermute only.
A program may use at most 128 MiB of HBM per device.

```python
import math
import jax
import jax.numpy as jnp
from jax import lax

L_DEG = 52
MPAD = 128
Q = 256
SHELLS = 64
TYPES = 8
ATOM_DEV = 1024
ATOMS = 131072
ROT = 512


def place_ends(result, rng, smallest, largest):
    spot = [jax.random.randint(jax.random.fold_in(rng, axis), (), 0, length) for axis, length in enumerate(result.shape)]
    main_axis = result.shape.index(max(result.shape))
    beside = spot[:main_axis] + [(spot[main_axis] + 1) % result.shape[main_axis]] + spot[main_axis + 1:]
    return result.at[tuple(spot)].set(smallest).at[tuple(beside)].set(largest)


def shard_levels(key, shape, split, least, largest):
    def one(dim, parts):
        steps = jax.random.uniform(jax.random.fold_in(jax.random.fold_in(key, 6), dim), (parts,), jnp.float32, least / len(split), largest / len(split))
        return jnp.repeat(jnp.exp(steps), shape[dim] // parts).reshape((-1,) + (1,) * (len(shape) - dim - 1))

    loudness = one(*split[0])
    for cut in split[1:]:
        loudness = loudness * one(*cut)
    return loudness


def gaussian(stream_key, extent, spread, limit, pieces=(), kind=jnp.bfloat16):
    loudness = shard_levels(stream_key, extent, pieces, -0.22, 0.18) if pieces else 1.0
    entries = jax.random.normal(stream_key, extent, jnp.float32) * spread * loudness
    return jnp.minimum(jnp.maximum(entries, -limit), limit).astype(kind)


def setup_inputs(seed: int = 0) -> dict:
    seeds = jax.random.split(jax.random.key(seed), 8)
    harmonic = gaussian(seeds[0], (ATOMS, L_DEG, MPAD), 1.0, 6.0, ((0, 128), (1, 2)))
    shell = place_ends(jax.random.randint(seeds[1], (ATOMS,), 0, SHELLS), jax.random.fold_in(seeds[1], 1), 0, SHELLS - 1).astype(jnp.int32)
    atom_type = place_ends(jax.random.randint(seeds[2], (ATOMS,), 0, TYPES), jax.random.fold_in(seeds[2], 1), 0, TYPES - 1).astype(jnp.int32)
    domain = place_ends(jax.random.randint(seeds[3], (ATOMS,), 0, 2), jax.random.fold_in(seeds[3], 1), 0, 1).astype(jnp.int32)
    form = jnp.clip(jnp.exp(jax.random.uniform(seeds[4], (TYPES, Q), jnp.float32, math.log(0.5), math.log(4.0))), 0.5, 4.0)
    bessel = jnp.clip(jax.random.uniform(seeds[5], (SHELLS, L_DEG, Q), jnp.float32, -1.0, 1.0) * shard_levels(seeds[5], (SHELLS, L_DEG, Q), ((1, 2),), -0.4, 0.0), -1.0, 1.0)
    wigner = gaussian(seeds[6], (ROT, L_DEG, MPAD, MPAD), MPAD ** -0.5, 0.5, ((0, 128), (1, 2)))
    return {"harmonic": harmonic, "shell": shell, "atom_type": atom_type, "domain": domain, "form": form, "bessel": bessel, "wigner": wigner}


def reference(harmonic, shell, atom_type, domain, form, bessel, wigner):
    keys_all = (domain * SHELLS + shell) * TYPES + atom_type
    nkeys = 2 * SHELLS * TYPES
    block = ATOM_DEV
    nblocks = ATOMS // block

    def add_block(total, index):
        start = (index * block).astype(jnp.int32)
        rows = lax.dynamic_slice_in_dim(harmonic, start, block, 0).astype(jnp.float32)
        keys = lax.dynamic_slice_in_dim(keys_all, start, block, 0)
        return (total + jax.ops.segment_sum(rows.reshape(block, -1), keys, nkeys), None)
    binned, _ = lax.scan(add_block, jnp.zeros((nkeys, L_DEG * MPAD), jnp.float32), jnp.arange(nblocks, dtype=jnp.int32))
    binned = binned.reshape(2, SHELLS * TYPES, L_DEG, MPAD)
    radial = (bessel[:, None, :, :] * form[None, :, None, :]).reshape(SHELLS * TYPES, L_DEG, Q)
    degree = jnp.arange(L_DEG, dtype=jnp.int32)
    mask = (jnp.arange(MPAD, dtype=jnp.int32)[None, :] < 2 * degree[:, None] + 1).astype(jnp.float32)
    amplitude = jnp.einsum('dklm,klq->qdlm', binned, radial, precision=lax.Precision.HIGHEST)
    amplitude = (amplitude * mask[None, None] / jnp.sqrt(jnp.float32(ATOMS))).astype(jnp.bfloat16)
    first = amplitude[:, 0].astype(jnp.float32)
    second = amplitude[:, 1].astype(jnp.float32)

    def one_rotation(blocks):
        turned = jnp.einsum('lmk,qlk->qlm', blocks.astype(jnp.float32), second)
        return lax.optimization_barrier(jnp.sum(first * turned, axis=(1, 2)))
    intensity = lax.map(one_rotation, wigner)
    return intensity / L_DEG
```

```python
import jax
import jax.numpy as jnp
from jax import lax
from jax.sharding import Mesh, PartitionSpec as P

SHELLS = 64
TYPES = 8
NEAR = ("y", "xl")
FAR = "z"


def widths(local_deg):
    rows = []
    for j in range(local_deg):
        live = 2 * (local_deg + j) + 1
        rows.append(-(-live // 16) * 16)
    return rows


def exchange(x, axis, parts):
    return lax.all_to_all(x.reshape(parts, x.shape[0] // parts, x.shape[1]), axis, 0, 0)


def spread(x, axis, parts):
    y = lax.all_to_all(jnp.broadcast_to(x[None], (parts,) + x.shape), axis, 0, 0)
    return y.reshape(parts * x.shape[0], x.shape[1])


def per_device(harmonic, shell, atom_type, domain, form, bessel, wigner):
    atom_rows, local_deg, width = harmonic.shape
    qcount = form.shape[1]
    total_atoms = atom_rows * 128
    nkeys = 2 * SHELLS * TYPES
    keys = (domain * SHELLS + shell) * TYPES + atom_type
    onehot = (keys[:, None] == jnp.arange(nkeys, dtype=jnp.int32)[None, :]).astype(jnp.bfloat16)
    binned = lax.dot_general(
        onehot,
        harmonic.reshape(atom_rows, local_deg * width),
        (((0,), (0,)), ((), ())),
        preferred_element_type=jnp.float32,
    )
    binned = binned.reshape(2, SHELLS * TYPES, local_deg, width)
    radial = (bessel[:, None, :, :] * form[None, :, None, :]).reshape(
        SHELLS * TYPES, local_deg, qcount
    )
    degree = lax.axis_index("deg") * local_deg + jnp.arange(local_deg, dtype=jnp.int32)
    mask = (jnp.arange(width, dtype=jnp.int32)[None, :] < 2 * degree[:, None] + 1).astype(
        jnp.float32
    )
    factor = mask[:, :, None, None] / jnp.sqrt(jnp.float32(total_atoms))
    term = jnp.einsum("dklm,klq->lmdq", binned, radial, precision=lax.Precision.HIGHEST)
    term = term * factor
    rows = widths(local_deg)
    live = sum(rows)
    total = -(-live // 256) * 256
    packed = jnp.concatenate(
        [term[j, :w] for j, w in enumerate(rows)]
        + [jnp.zeros((total - live, 2, qcount), jnp.float32)],
        axis=0,
    )
    core = lax.axis_index("c")
    swap = [(0, 1), (1, 0)]
    keep = jnp.where(core == 0, packed[:, 0], packed[:, 1])
    give = jnp.where(core == 0, packed[:, 1], packed[:, 0])
    part = keep + lax.ppermute(give, "c", swap)
    part = jnp.sum(exchange(part, NEAR, 8), axis=0)
    half = qcount // 2
    part = jnp.concatenate([part[:, :half], part[:, half:]], axis=0)
    part = jnp.sum(exchange(part, FAR, 8), axis=0)
    part = part.astype(jnp.bfloat16)
    part = spread(part, FAR, 8)
    deep = part.shape[0] // 2
    part = jnp.concatenate([part[:deep], part[deep:]], axis=1)
    mine = spread(part, NEAR, 8)
    other = lax.ppermute(mine, "c", swap)
    first = jnp.where(core == 0, mine, other)
    second = jnp.where(core == 0, other, mine)
    out = jnp.zeros((wigner.shape[0], qcount), jnp.float32)
    start = 0
    for j, w in enumerate(rows):
        a0 = first[start : start + w].astype(jnp.float32)
        a1 = second[start : start + w]
        turned = jnp.einsum(
            "rmk,kq->rmq", wigner[:, j, :w, :w], a1, preferred_element_type=jnp.float32
        )
        out = out + jnp.sum(a0[None] * turned, axis=1)
        start += w
    return lax.psum(out, "deg") / (2 * local_deg)


def solution(mesh):
    grid = Mesh(mesh.devices.reshape(4, 2, 8, 2, 2), ("y", "xl", "z", "c", "deg"))
    slab = ("y", "xl", "z", "c")
    in_specs = (
        P(slab, "deg", None),
        P(slab),
        P(slab),
        P(slab),
        P(),
        P(None, "deg", None),
        P(slab, "deg", None, None),
    )
    return jax.shard_map(
        per_device, mesh=grid, in_specs=in_specs, out_specs=P(slab, None), check_vma=False
    )
```

```python
import functools
import jax
import jax.numpy as jnp
from jax import lax
from jax.experimental import pallas as pl
from jax.experimental.pallas import tpu as pltpu
from jax.sharding import Mesh, PartitionSpec as P

SHELLS = 64
TYPES = 8
BINS = SHELLS * TYPES
NEAR = ("y", "xl")
FAR = "z"


def widths(local_deg):
    return [-(-(2 * (local_deg + j) + 1) // 16) * 16 for j in range(local_deg)]


def start_of(local, rows):
    return sum(jnp.where(local > j, w, 0) for j, w in enumerate(rows[:-1]))


def wide_of(local, rows):
    cuts = [j for j in range(1, len(rows)) if rows[j] != rows[j - 1]]
    return rows[0] + sum(jnp.where(local >= j, rows[j] - rows[j - 1], 0) for j in cuts)


def contract_first(a, b):
    return lax.dot_general(a, b, (((0,), (0,)), ((), ())), preferred_element_type=jnp.float32)


def amplitude_kernel(pair, scale, rows, place, keys, harmonic, bessel, form, keep, give, onehot):
    step = pl.program_id(0)

    @pl.when(step == 0)
    def _():
        slots = lax.broadcasted_iota(jnp.int32, onehot.shape, 0)
        onehot[...] = jnp.where(slots == keys[...], 1.0, 0.0).astype(jnp.bfloat16)
        keep[...] = jnp.zeros_like(keep)
        give[...] = jnp.zeros_like(give)

    both = jnp.concatenate([harmonic[i] for i in range(pair)], axis=1)
    binned = jnp.dot(onehot[...], both, preferred_element_type=jnp.float32)
    width = harmonic.shape[2]
    for i in range(pair):
        mine = binned[:, i * width : (i + 1) * width]
        cols = jnp.concatenate([mine[:BINS], mine[BINS:]], axis=1)
        cols_hi = cols.astype(jnp.bfloat16)
        cols_lo = (cols - cols_hi.astype(jnp.float32)).astype(jnp.bfloat16)
        radial = (bessel[i][:, None, :] * form[...][None]).reshape(BINS, form.shape[1])
        radial_hi = radial.astype(jnp.bfloat16)
        radial_lo = (radial - radial_hi.astype(jnp.float32)).astype(jnp.bfloat16)
        out = contract_first(cols_hi, radial_hi)
        out = out + contract_first(cols_lo, radial_hi)
        out = out + contract_first(cols_hi, radial_lo)
        local = step * pair + i
        live = 2 * (place[0] + local) + 1
        order = lax.broadcasted_iota(jnp.int32, (width, out.shape[1]), 0)
        at = pl.ds(pl.multiple_of(start_of(local, rows), 16), width)
        keep[at, :] = jnp.where(order < live, out[:width] * scale, 0.0)
        give[at, :] = jnp.where(order < live, out[width:] * scale, 0.0)


def local_amplitude(place, keys, harmonic, bessel, form, total, pair, scale, rows):
    degs, atoms, width = harmonic.shape
    qcount = form.shape[1]
    out = jax.ShapeDtypeStruct((total, qcount), jnp.float32)
    grid_spec = pltpu.PrefetchScalarGridSpec(
        num_scalar_prefetch=1,
        grid=(degs // pair,),
        in_specs=[
            pl.BlockSpec((1, atoms), lambda s, *_: (0, 0)),
            pl.BlockSpec((pair, atoms, width), lambda s, *_: (s, 0, 0)),
            pl.BlockSpec((pair, SHELLS, qcount), lambda s, *_: (s, 0, 0)),
            pl.BlockSpec((TYPES, qcount), lambda s, *_: (0, 0)),
        ],
        out_specs=[pl.BlockSpec((total, qcount), lambda s, *_: (0, 0))] * 2,
        scratch_shapes=[pltpu.VMEM((2 * BINS, atoms), jnp.bfloat16)],
    )
    return pl.pallas_call(
        functools.partial(amplitude_kernel, pair, scale, rows),
        grid_spec=grid_spec,
        out_shape=[out, out],
        compiler_params=pltpu.CompilerParams(vmem_limit_bytes=40 * 2**20),
        cost_estimate=pl.CostEstimate(
            flops=2 * degs * width * (2 * BINS * atoms + 6 * BINS * qcount),
            bytes_accessed=harmonic.size * 2 + bessel.size * 4,
            transcendentals=0,
        ),
    )(place, keys, harmonic, bessel, form)


def turn_kernel(group, steps, rows, place, mine, other, wigner, out, acc):
    step = pl.program_id(0)
    rots, width = wigner.shape[0], wigner.shape[2]
    qcount = mine.shape[1]

    @pl.when(step == 0)
    def _():
        acc[...] = jnp.zeros_like(acc)

    order = lax.broadcasted_iota(jnp.int32, (width, qcount), 0)
    swap = jnp.broadcast_to(place[1], (width, qcount)) == 1
    for i in range(group):
        local = step * group + i
        at = pl.ds(pl.multiple_of(start_of(local, rows), 16), width)
        inside = order < wide_of(local, rows)
        here = jnp.where(inside, mine[at, :].astype(jnp.float32), 0.0)
        there = jnp.where(inside, other[at, :].astype(jnp.float32), 0.0)
        first = jnp.where(swap, there, here)
        second = jnp.where(swap, here, there).astype(jnp.bfloat16)
        blocks = wigner[:, i].reshape(rots * width, width)
        turned = jnp.dot(blocks, second, preferred_element_type=jnp.float32)
        for r in range(rots):
            prod = turned[r * width : (r + 1) * width] * first
            acc[r] += jnp.sum(prod.reshape(width // 8, 8, qcount), axis=0)

    @pl.when(step == steps - 1)
    def _():
        out[...] = jnp.sum(acc[...], axis=1) * (0.5 / (steps * group))


def local_intensity(place, mine, other, wigner, group, rows):
    rots, degs, width, _ = wigner.shape
    total, qcount = mine.shape
    grid_spec = pltpu.PrefetchScalarGridSpec(
        num_scalar_prefetch=1,
        grid=(degs // group,),
        in_specs=[
            pl.BlockSpec((total, qcount), lambda s, *_: (0, 0)),
            pl.BlockSpec((total, qcount), lambda s, *_: (0, 0)),
            pl.BlockSpec((rots, group, width, width), lambda s, *_: (0, s, 0, 0)),
        ],
        out_specs=pl.BlockSpec((rots, qcount), lambda s, *_: (0, 0)),
        scratch_shapes=[pltpu.VMEM((rots, 8, qcount), jnp.float32)],
    )
    return pl.pallas_call(
        functools.partial(turn_kernel, group, degs // group, rows),
        grid_spec=grid_spec,
        out_shape=jax.ShapeDtypeStruct((rots, qcount), jnp.float32),
        compiler_params=pltpu.CompilerParams(vmem_limit_bytes=40 * 2**20),
        cost_estimate=pl.CostEstimate(
            flops=2 * wigner.size * qcount,
            bytes_accessed=wigner.size * 2 + mine.size * 4,
            transcendentals=0,
        ),
    )(place, mine, other, wigner)


def coded(x, spare):
    top = jnp.maximum(jnp.max(jnp.abs(x), axis=0, keepdims=True), 1e-30)
    power = jnp.floor(jnp.log2(top)) + 1.0
    steps = jnp.clip(jnp.round(x * jnp.exp2(15.0 - power)), -32767.0, 32767.0)
    tail = jnp.broadcast_to(power, (spare, x.shape[1]))
    return jnp.concatenate([steps, tail], axis=0).astype(jnp.int32).astype(jnp.int16)


def decoded(block, rows):
    wide = block.astype(jnp.int32).astype(jnp.float32)
    return wide[:rows] * jnp.exp2(wide[rows : rows + 1] - 15.0)


def near_kernel(keep, recv, out):
    out[0] = coded(keep[...] + recv[...], out.shape[1] - keep.shape[0])


def far_kernel(parts, rows, near, out):
    total = decoded(near[0], rows)
    for i in range(1, near.shape[0]):
        total = total + decoded(near[i], rows)
    half = total.shape[1] // 2
    piece = rows * 2 // parts
    for i in range(parts):
        side, row = divmod(i * piece, rows)
        block = total[row : row + piece, side * half : (side + 1) * half]
        out[i] = coded(block, out.shape[1] - piece)


def last_kernel(far, out):
    total = decoded(far[0], out.shape[0])
    for i in range(1, far.shape[0]):
        total = total + decoded(far[i], out.shape[0])
    out[...] = total


def near_parts(keep, recv, parts):
    total, lanes = keep.shape
    rows = total // parts
    spare = 32 - rows % 16 if rows % 16 else 16
    return pl.pallas_call(
        near_kernel,
        grid=(parts,),
        in_specs=[pl.BlockSpec((rows, lanes), lambda s: (s, 0))] * 2,
        out_specs=pl.BlockSpec((1, rows + spare, lanes), lambda s: (s, 0, 0)),
        out_shape=jax.ShapeDtypeStruct((parts, rows + spare, lanes), jnp.int16),
    )(keep, recv), rows


def far_parts(near, rows, parts):
    piece = rows * 2 // parts
    return pl.pallas_call(
        functools.partial(far_kernel, parts, rows),
        out_shape=jax.ShapeDtypeStruct((parts, piece + 8, near.shape[2] // 2), jnp.int16),
        compiler_params=pltpu.CompilerParams(vmem_limit_bytes=40 * 2**20),
    )(near), piece


def last_sum(far, piece):
    return pl.pallas_call(
        last_kernel,
        out_shape=jax.ShapeDtypeStruct((piece, far.shape[2]), jnp.float32),
    )(far)


def exchange(x, axis):
    return lax.all_to_all(x, axis, 0, 0)


def spread(x, axis, parts):
    y = lax.all_to_all(jnp.broadcast_to(x[None], (parts,) + x.shape), axis, 0, 0)
    return y.reshape(parts * x.shape[0], x.shape[1])


def per_device(harmonic, shell, atom_type, domain, form, bessel, wigner):
    atom_rows, local_deg, width = harmonic.shape
    rows = widths(local_deg)
    total = -(-sum(rows) // 256) * 256
    core = lax.axis_index("c")
    swap = [(0, 1), (1, 0)]
    place = jnp.stack([lax.axis_index("deg") * local_deg, core]).astype(jnp.int32)
    side = jnp.where(core == 0, domain, 1 - domain)
    keys = ((side * SHELLS + shell) * TYPES + atom_type)[None]
    keep, give = local_amplitude(
        place,
        keys,
        harmonic.transpose(1, 0, 2),
        bessel.transpose(1, 0, 2),
        form,
        total,
        2,
        (atom_rows * 128) ** -0.5,
        rows,
    )
    near, height = near_parts(keep, lax.ppermute(give, "c", swap), 8)
    far, piece = far_parts(exchange(near, NEAR), height, 8)
    part = last_sum(exchange(far, FAR), piece).astype(jnp.bfloat16)
    part = spread(part, FAR, 8)
    deep = part.shape[0] // 2
    part = jnp.concatenate([part[:deep], part[deep:]], axis=1)
    mine = spread(part, NEAR, 8)
    other = lax.ppermute(mine, "c", swap)
    out = local_intensity(place, mine, other, wigner, 2, rows)
    return out + lax.ppermute(out, "deg", swap)


def solution(mesh):
    grid = Mesh(mesh.devices.reshape(4, 2, 8, 2, 2), ("y", "xl", "z", "c", "deg"))
    slab = ("y", "xl", "z", "c")
    in_specs = (
        P(slab, "deg", None),
        P(slab),
        P(slab),
        P(slab),
        P(),
        P(None, "deg", None),
        P(slab, "deg", None, None),
    )
    return jax.shard_map(
        per_device, mesh=grid, in_specs=in_specs, out_specs=P(slab, None), check_vma=False
    )
```

```python
import functools
import jax
import jax.numpy as jnp
from jax import lax
from jax.experimental import pallas as pl
from jax.experimental.pallas import tpu as pltpu
from jax.sharding import Mesh, PartitionSpec as P

SHELLS = 64
TYPES = 8
BINS = SHELLS * TYPES
NEAR = ("y", "xl", "zl")
FAR = "zh"
PLANE = 16
LIMIT = 8


def widths(local_deg):
    return [-(-(2 * (local_deg + j) + 1) // 16) * 16 for j in range(local_deg)]


def start_of(local, rows):
    return sum(jnp.where(local > j, w, 0) for j, w in enumerate(rows[:-1]))


def wide_of(local, rows):
    cuts = [j for j in range(1, len(rows)) if rows[j] != rows[j - 1]]
    return rows[0] + sum(jnp.where(local >= j, rows[j] - rows[j - 1], 0) for j in cuts)


def contract_first(a, b):
    return lax.dot_general(a, b, (((0,), (0,)), ((), ())), preferred_element_type=jnp.float32)


def amplitude_kernel(pair, scale, rows, place, keys, harmonic, bessel, form, keep, give, onehot):
    step = pl.program_id(0)

    @pl.when(step == 0)
    def _():
        slots = lax.broadcasted_iota(jnp.int32, onehot.shape, 0)
        onehot[...] = jnp.where(slots == keys[...], 1.0, 0.0).astype(jnp.bfloat16)
        keep[...] = jnp.zeros_like(keep)
        give[...] = jnp.zeros_like(give)

    both = jnp.concatenate([harmonic[i] for i in range(pair)], axis=1)
    binned = jnp.dot(onehot[...], both, preferred_element_type=jnp.float32)
    width = harmonic.shape[2]
    for i in range(pair):
        mine = binned[:, i * width : (i + 1) * width]
        cols = jnp.concatenate([mine[:BINS], mine[BINS:]], axis=1)
        cols_hi = cols.astype(jnp.bfloat16)
        cols_lo = (cols - cols_hi.astype(jnp.float32)).astype(jnp.bfloat16)
        radial = (bessel[i][:, None, :] * form[...][None]).reshape(BINS, form.shape[1])
        radial_hi = radial.astype(jnp.bfloat16)
        radial_lo = (radial - radial_hi.astype(jnp.float32)).astype(jnp.bfloat16)
        out = contract_first(cols_hi, radial_hi)
        out = out + contract_first(cols_lo, radial_hi)
        out = out + contract_first(cols_hi, radial_lo)
        local = step * pair + i
        live = 2 * (place[0] + local) + 1
        order = lax.broadcasted_iota(jnp.int32, (width, out.shape[1]), 0)
        at = pl.ds(pl.multiple_of(start_of(local, rows), 16), width)
        keep[at, :] = jnp.where(order < live, out[:width] * scale, 0.0)
        give[at, :] = jnp.where(order < live, out[width:] * scale, 0.0)


def local_amplitude(place, keys, harmonic, bessel, form, total, pair, scale, rows):
    degs, atoms, width = harmonic.shape
    qcount = form.shape[1]
    out = jax.ShapeDtypeStruct((total, qcount), jnp.float32)
    grid_spec = pltpu.PrefetchScalarGridSpec(
        num_scalar_prefetch=1,
        grid=(degs // pair,),
        in_specs=[
            pl.BlockSpec((1, atoms), lambda s, *_: (0, 0)),
            pl.BlockSpec((pair, atoms, width), lambda s, *_: (s, 0, 0)),
            pl.BlockSpec((pair, SHELLS, qcount), lambda s, *_: (s, 0, 0)),
            pl.BlockSpec((TYPES, qcount), lambda s, *_: (0, 0)),
        ],
        out_specs=[pl.BlockSpec(memory_space=pltpu.VMEM)] * 2,
        scratch_shapes=[pltpu.VMEM((2 * BINS, atoms), jnp.bfloat16)],
    )
    return pl.pallas_call(
        functools.partial(amplitude_kernel, pair, scale, rows),
        grid_spec=grid_spec,
        out_shape=[out, out],
        compiler_params=pltpu.CompilerParams(vmem_limit_bytes=56 * 2**20),
        cost_estimate=pl.CostEstimate(
            flops=2 * degs * width * (2 * BINS * atoms + 6 * BINS * qcount),
            bytes_accessed=harmonic.size * 2 + bessel.size * 4,
            transcendentals=0,
        ),
    )(place, keys, harmonic, bessel, form)


def turn_kernel(group, steps, rows, place, mine, other, wigner, out, acc):
    step = pl.program_id(0)
    rots, width = wigner.shape[0], wigner.shape[2]
    qcount = mine.shape[1]

    @pl.when(step == 0)
    def _():
        acc[...] = jnp.zeros_like(acc)

    order = lax.broadcasted_iota(jnp.int32, (width, qcount), 0)
    swap = jnp.broadcast_to(place[1], (width, qcount)) == 1
    for i in range(group):
        local = step * group + i
        at = pl.ds(pl.multiple_of(start_of(local, rows), 16), width)
        inside = order < wide_of(local, rows)
        here = jnp.where(inside, mine[at, :].astype(jnp.float32), 0.0)
        there = jnp.where(inside, other[at, :].astype(jnp.float32), 0.0)
        first = jnp.where(swap, there, here)
        second = jnp.where(swap, here, there).astype(jnp.bfloat16)
        blocks = wigner[:, i].reshape(rots * width, width)
        turned = jnp.dot(blocks, second, preferred_element_type=jnp.float32)
        for r in range(rots):
            prod = turned[r * width : (r + 1) * width] * first
            acc[r] += jnp.sum(prod.reshape(width // 8, 8, qcount), axis=0)

    @pl.when(step == steps - 1)
    def _():
        out[...] = jnp.sum(acc[...], axis=1) * (0.5 / (steps * group))


def local_intensity(place, mine, other, wigner, group, rows):
    rots, degs, width, _ = wigner.shape
    total, qcount = mine.shape
    grid_spec = pltpu.PrefetchScalarGridSpec(
        num_scalar_prefetch=1,
        grid=(degs // group,),
        in_specs=[
            pl.BlockSpec((total, qcount), lambda s, *_: (0, 0)),
            pl.BlockSpec((total, qcount), lambda s, *_: (0, 0)),
            pl.BlockSpec((rots, group, width, width), lambda s, *_: (0, s, 0, 0)),
        ],
        out_specs=pl.BlockSpec((rots, qcount), lambda s, *_: (0, 0)),
        scratch_shapes=[pltpu.VMEM((rots, 8, qcount), jnp.float32)],
    )
    return pl.pallas_call(
        functools.partial(turn_kernel, group, degs // group, rows),
        grid_spec=grid_spec,
        out_shape=jax.ShapeDtypeStruct((rots, qcount), jnp.float32),
        compiler_params=pltpu.CompilerParams(vmem_limit_bytes=40 * 2**20),
        cost_estimate=pl.CostEstimate(
            flops=2 * wigner.size * qcount,
            bytes_accessed=wigner.size * 2 + mine.size * 4,
            transcendentals=0,
        ),
    )(place, mine, other, wigner)


def coded(x, spare):
    top = jnp.maximum(jnp.max(jnp.abs(x), axis=0, keepdims=True), 1e-30)
    power = jnp.floor(jnp.log2(top)) + 1.0
    steps = jnp.clip(jnp.round(x * jnp.exp2(15.0 - power)), -32767.0, 32767.0)
    tail = jnp.broadcast_to(power, (spare, x.shape[1]))
    return jnp.concatenate([steps, tail], axis=0).astype(jnp.int32).astype(jnp.int16)


def decoded(block, rows):
    wide = block.astype(jnp.int32).astype(jnp.float32)
    return wide[:rows] * jnp.exp2(wide[rows : rows + 1] - 15.0)


def near_kernel(rows, keep, recv, out):
    for i in range(out.shape[0]):
        at = pl.ds(i * rows, rows)
        out[i] = coded(keep[at, :] + recv[at, :], out.shape[1] - rows)


def plane_kernel(rows, near, total, code):
    acc = decoded(near[0], rows)
    for i in range(1, near.shape[0]):
        acc = acc + decoded(near[i], rows)
    total[...] = acc
    code[...] = coded(acc, code.shape[0] - rows)


def whole_kernel(total, after, before, across, out):
    rows = total.shape[0]
    acc = total[...] + decoded(across[...], rows)
    acc = acc + (decoded(after[...], rows) + decoded(before[...], rows))
    block = acc.astype(jnp.bfloat16)
    for i in range(out.shape[0]):
        out[i] = block


def whole_call(body, out_shape, limit, *args):
    spec = pl.BlockSpec(memory_space=pltpu.VMEM)
    return pl.pallas_call(
        body,
        in_specs=[spec] * len(args),
        out_specs=jax.tree.map(lambda _: spec, out_shape),
        out_shape=out_shape,
        compiler_params=pltpu.CompilerParams(vmem_limit_bytes=limit * 2**20),
    )(*args)


def per_device(harmonic, shell, atom_type, domain, form, bessel, wigner):
    atom_rows, local_deg, width = harmonic.shape
    qcount = form.shape[1]
    rows = widths(local_deg)
    total = -(-sum(rows) // 256) * 256
    core = lax.axis_index("c")
    swap = [(0, 1), (1, 0)]
    place = jnp.stack([lax.axis_index("deg") * local_deg, core]).astype(jnp.int32)
    side = jnp.where(core == 0, domain, 1 - domain)
    keys = ((side * SHELLS + shell) * TYPES + atom_type)[None]
    keep, give = local_amplitude(
        place,
        keys,
        harmonic.transpose(1, 0, 2),
        bessel.transpose(1, 0, 2),
        form,
        total,
        2,
        (atom_rows * 128) ** -0.5,
        rows,
    )
    recv = lax.ppermute(give, "c", swap)
    height = total // PLANE
    coded_shape = (height + 16, qcount)
    near = whole_call(
        functools.partial(near_kernel, height),
        jax.ShapeDtypeStruct((PLANE,) + coded_shape, jnp.int16),
        LIMIT,
        keep,
        recv,
    )
    near = lax.all_to_all(near, NEAR, 0, 0)
    part, code = whole_call(
        functools.partial(plane_kernel, height),
        [
            jax.ShapeDtypeStruct((height, qcount), jnp.float32),
            jax.ShapeDtypeStruct(coded_shape, jnp.int16),
        ],
        LIMIT,
        near,
    )
    turns = [lax.ppermute(code, FAR, [(i, (i + k) % 4) for i in range(4)]) for k in (1, 3, 2)]
    spread = whole_call(
        whole_kernel,
        jax.ShapeDtypeStruct((PLANE, height, qcount), jnp.bfloat16),
        LIMIT,
        part,
        *turns,
    )
    mine = lax.all_to_all(spread, NEAR, 0, 0).reshape(total, qcount)
    other = lax.ppermute(mine, "c", swap)
    out = local_intensity(place, mine, other, wigner, 2, rows)
    return out + lax.ppermute(out, "deg", swap)


def solution(mesh):
    grid = Mesh(mesh.devices.reshape(4, 2, 4, 2, 2, 2), ("y", "xl", "zh", "zl", "c", "deg"))
    slab = ("y", "xl", "zh", "zl", "c")
    in_specs = (
        P(slab, "deg", None),
        P(slab),
        P(slab),
        P(slab),
        P(),
        P(None, "deg", None),
        P(slab, "deg", None, None),
    )
    return jax.shard_map(
        per_device, mesh=grid, in_specs=in_specs, out_specs=P(slab, None), check_vma=False
    )
```

```python
import functools
import jax
import jax.numpy as jnp
from jax import lax
from jax.experimental import pallas as pl
from jax.experimental.pallas import tpu as pltpu
from jax.sharding import Mesh, PartitionSpec as P

SHELLS = 64
TYPES = 8
BINS = SHELLS * TYPES
NEAR = ("y", "xl", "zl")
FAR = "zh"
PLANE = 16
LIMIT = 8
CHUNK = 1120


def widths(local_deg):
    return [-(-(2 * (local_deg + j) + 1) // 16) * 16 for j in range(local_deg)]


def start_of(local, rows):
    return sum(jnp.where(local > j, w, 0) for j, w in enumerate(rows[:-1]))


def wide_of(local, rows):
    cuts = [j for j in range(1, len(rows)) if rows[j] != rows[j - 1]]
    return rows[0] + sum(jnp.where(local >= j, rows[j] - rows[j - 1], 0) for j in cuts)


def runs_of(rows):
    runs, at = [], 0
    for j, w in enumerate(rows):
        if runs and runs[-1][2] == w:
            runs[-1][1] += 1
        else:
            runs.append([j, 1, w, at])
        at += w
    return runs


def amplitude_kernel(
    scale, rows, place, keys, harmonic, bessel, form, keep, give,
    atoms, waves, onehot, turned, high, low, atom_sems, wave_sem,
):
    live_rows = sum(rows)
    width = harmonic.shape[2]
    qcount = form.shape[1]
    fetch = [
        pltpu.make_async_copy(harmonic.at[j], atoms.at[j], atom_sems.at[j])
        for j in range(len(rows))
    ]
    for copy in fetch:
        copy.start()
    wave_copy = pltpu.make_async_copy(bessel, waves, wave_sem)
    wave_copy.start()

    slots = lax.broadcasted_iota(jnp.int32, (width, 2 * BINS), 1).astype(jnp.float32)
    for i in range(atoms.shape[1] // width):
        line = keys[:, i * width : (i + 1) * width].astype(jnp.float32)
        tall = jnp.transpose(jnp.broadcast_to(line, (width, width)))
        same = slots == jnp.concatenate([tall] * (2 * BINS // width), axis=1)
        onehot[i * width : (i + 1) * width, :] = jnp.where(same, 1.0, 0.0).astype(jnp.bfloat16)
    tail = keep.shape[0] - live_rows
    keep[live_rows:, :] = jnp.zeros((tail, qcount), jnp.float32)
    give[live_rows:, :] = jnp.zeros((tail, qcount), jnp.float32)

    for first, count, wide, at in runs_of(rows):

        def turn(j, carry):
            pltpu.make_async_copy(
                harmonic.at[first + j], atoms.at[first + j], atom_sems.at[first + j]
            ).wait()
            there = pl.ds(pl.multiple_of(at + j * wide, 16), wide)
            turned[there, :] = jnp.transpose(atoms[first + j])[:wide]
            return carry

        lax.fori_loop(0, count, turn, 0)

    chunk = CHUNK

    def bin_rows(i, carry):
        there = pl.ds(pl.multiple_of(i * chunk, 16), chunk)
        binned = jnp.dot(turned[there, :], onehot[...], preferred_element_type=jnp.float32)
        top = binned.astype(jnp.bfloat16)
        high[there, :] = top
        low[there, :] = (binned - top.astype(jnp.float32)).astype(jnp.bfloat16)
        return carry

    lax.fori_loop(0, live_rows // chunk, bin_rows, 0)
    wave_copy.wait()

    for first, count, wide, at in runs_of(rows):

        def mix(j, carry):
            radial = (waves[first + j][:, None, :] * form[...][None]).reshape(BINS, qcount)
            radial_hi = radial.astype(jnp.bfloat16)
            radial_lo = (radial - radial_hi.astype(jnp.float32)).astype(jnp.bfloat16)
            there = pl.ds(pl.multiple_of(at + j * wide, 16), wide)
            tops = [high[there, :BINS], high[there, BINS:]]
            lows = [low[there, :BINS], low[there, BINS:]]
            main = jnp.dot(
                jnp.concatenate(tops + lows, axis=0),
                radial_hi,
                preferred_element_type=jnp.float32,
            )
            rest = jnp.dot(
                jnp.concatenate(tops, axis=0), radial_lo, preferred_element_type=jnp.float32
            )
            out = (main[: 2 * wide] + (main[2 * wide :] + rest)) * scale
            live = 2 * (place[0] + first + j) + 1
            order = lax.broadcasted_iota(jnp.int32, (wide, qcount), 0)
            keep[there, :] = jnp.where(order < live, out[:wide], 0.0)
            give[there, :] = jnp.where(order < live, out[wide:], 0.0)
            return carry

        for j in range(count):
            mix(j, 0)


def local_amplitude(place, keys, harmonic, bessel, form, total, scale, rows):
    degs, atoms, width = harmonic.shape
    qcount = form.shape[1]
    live_rows = sum(rows)
    out = jax.ShapeDtypeStruct((total, qcount), jnp.float32)
    return pl.pallas_call(
        functools.partial(amplitude_kernel, scale, rows),
        in_specs=[
            pl.BlockSpec(memory_space=pltpu.SMEM),
            pl.BlockSpec(memory_space=pltpu.VMEM),
            pl.BlockSpec(memory_space=pltpu.HBM),
            pl.BlockSpec(memory_space=pltpu.HBM),
            pl.BlockSpec(memory_space=pltpu.VMEM),
        ],
        out_specs=[pl.BlockSpec(memory_space=pltpu.VMEM)] * 2,
        out_shape=[out, out],
        scratch_shapes=[
            pltpu.VMEM((degs, atoms, width), jnp.bfloat16),
            pltpu.VMEM(bessel.shape, jnp.float32),
            pltpu.VMEM((atoms, 2 * BINS), jnp.bfloat16),
            pltpu.VMEM((live_rows, atoms), jnp.bfloat16),
            pltpu.VMEM((live_rows, 2 * BINS), jnp.bfloat16),
            pltpu.VMEM((live_rows, 2 * BINS), jnp.bfloat16),
            pltpu.SemaphoreType.DMA((degs,)),
            pltpu.SemaphoreType.DMA,
        ],
        compiler_params=pltpu.CompilerParams(vmem_limit_bytes=52 * 2**20),
        cost_estimate=pl.CostEstimate(
            flops=2 * live_rows * (2 * BINS * atoms + 6 * BINS * qcount),
            bytes_accessed=harmonic.size * 2 + bessel.size * 4,
            transcendentals=0,
        ),
    )(place, keys, harmonic, bessel, form)


def turn_kernel(group, steps, rows, place, mine, other, wigner, out, acc):
    step = pl.program_id(0)
    rots, width = wigner.shape[0], wigner.shape[2]
    qcount = mine.shape[1]

    @pl.when(step == 0)
    def _():
        acc[...] = jnp.zeros_like(acc)

    order = lax.broadcasted_iota(jnp.int32, (width, qcount), 0)
    swap = jnp.broadcast_to(place[1], (width, qcount)) == 1
    for i in range(group):
        local = step * group + i
        at = pl.ds(pl.multiple_of(start_of(local, rows), 16), width)
        inside = order < wide_of(local, rows)
        here = jnp.where(inside, mine[at, :].astype(jnp.float32), 0.0)
        there = jnp.where(inside, other[at, :].astype(jnp.float32), 0.0)
        first = jnp.where(swap, there, here)
        second = jnp.where(swap, here, there).astype(jnp.bfloat16)
        blocks = wigner[:, i].reshape(rots * width, width)
        turned = jnp.dot(blocks, second, preferred_element_type=jnp.float32)
        for r in range(rots):
            prod = turned[r * width : (r + 1) * width] * first
            acc[r] += jnp.sum(prod.reshape(width // 8, 8, qcount), axis=0)

    @pl.when(step == steps - 1)
    def _():
        out[...] = jnp.sum(acc[...], axis=1) * (0.5 / (steps * group))


def local_intensity(place, mine, other, wigner, group, rows):
    rots, degs, width, _ = wigner.shape
    total, qcount = mine.shape
    grid_spec = pltpu.PrefetchScalarGridSpec(
        num_scalar_prefetch=1,
        grid=(degs // group,),
        in_specs=[
            pl.BlockSpec((total, qcount), lambda s, *_: (0, 0)),
            pl.BlockSpec((total, qcount), lambda s, *_: (0, 0)),
            pl.BlockSpec((rots, group, width, width), lambda s, *_: (0, s, 0, 0)),
        ],
        out_specs=pl.BlockSpec((rots, qcount), lambda s, *_: (0, 0)),
        scratch_shapes=[pltpu.VMEM((rots, 8, qcount), jnp.float32)],
    )
    return pl.pallas_call(
        functools.partial(turn_kernel, group, degs // group, rows),
        grid_spec=grid_spec,
        out_shape=jax.ShapeDtypeStruct((rots, qcount), jnp.float32),
        compiler_params=pltpu.CompilerParams(vmem_limit_bytes=40 * 2**20),
        cost_estimate=pl.CostEstimate(
            flops=2 * wigner.size * qcount,
            bytes_accessed=wigner.size * 2 + mine.size * 4,
            transcendentals=0,
        ),
    )(place, mine, other, wigner)


def coded(x, spare):
    top = jnp.maximum(jnp.max(jnp.abs(x), axis=0, keepdims=True), 1e-30)
    power = jnp.floor(jnp.log2(top)) + 1.0
    steps = jnp.clip(jnp.round(x * jnp.exp2(15.0 - power)), -32767.0, 32767.0)
    tail = jnp.broadcast_to(power, (spare, x.shape[1]))
    return jnp.concatenate([steps, tail], axis=0).astype(jnp.int32).astype(jnp.int16)


def decoded(block, rows):
    wide = block.astype(jnp.int32).astype(jnp.float32)
    return wide[:rows] * jnp.exp2(wide[rows : rows + 1] - 15.0)


def near_kernel(rows, keep, recv, out):
    for i in range(out.shape[0]):
        at = pl.ds(i * rows, rows)
        out[i] = coded(keep[at, :] + recv[at, :], out.shape[1] - rows)


def plane_kernel(rows, near, total, code):
    acc = decoded(near[0], rows)
    for i in range(1, near.shape[0]):
        acc = acc + decoded(near[i], rows)
    total[...] = acc
    code[...] = coded(acc, code.shape[0] - rows)


def whole_kernel(total, after, before, across, out):
    rows = total.shape[0]
    acc = total[...] + decoded(across[...], rows)
    acc = acc + (decoded(after[...], rows) + decoded(before[...], rows))
    block = acc.astype(jnp.bfloat16)
    for i in range(out.shape[0]):
        out[i] = block


def whole_call(body, out_shape, limit, *args):
    spec = pl.BlockSpec(memory_space=pltpu.VMEM)
    return pl.pallas_call(
        body,
        in_specs=[spec] * len(args),
        out_specs=jax.tree.map(lambda _: spec, out_shape),
        out_shape=out_shape,
        compiler_params=pltpu.CompilerParams(vmem_limit_bytes=limit * 2**20),
    )(*args)


def per_device(harmonic, shell, atom_type, domain, form, bessel, wigner):
    atom_rows, local_deg, width = harmonic.shape
    qcount = form.shape[1]
    rows = widths(local_deg)
    total = -(-sum(rows) // 256) * 256
    core = lax.axis_index("c")
    swap = [(0, 1), (1, 0)]
    place = jnp.stack([lax.axis_index("deg") * local_deg, core]).astype(jnp.int32)
    side = jnp.where(core == 0, domain, 1 - domain)
    keys = ((side * SHELLS + shell) * TYPES + atom_type)[None]
    keep, give = local_amplitude(
        place,
        keys,
        harmonic.transpose(1, 0, 2),
        bessel.transpose(1, 0, 2),
        form,
        total,
        (atom_rows * 128) ** -0.5,
        rows,
    )
    recv = lax.ppermute(give, "c", swap)
    height = total // PLANE
    coded_shape = (height + 16, qcount)
    near = whole_call(
        functools.partial(near_kernel, height),
        jax.ShapeDtypeStruct((PLANE,) + coded_shape, jnp.int16),
        LIMIT,
        keep,
        recv,
    )
    near = lax.all_to_all(near, NEAR, 0, 0)
    part, code = whole_call(
        functools.partial(plane_kernel, height),
        [
            jax.ShapeDtypeStruct((height, qcount), jnp.float32),
            jax.ShapeDtypeStruct(coded_shape, jnp.int16),
        ],
        LIMIT,
        near,
    )
    turns = [lax.ppermute(code, FAR, [(i, (i + k) % 4) for i in range(4)]) for k in (1, 3, 2)]
    spread = whole_call(
        whole_kernel,
        jax.ShapeDtypeStruct((PLANE, height, qcount), jnp.bfloat16),
        LIMIT,
        part,
        *turns,
    )
    mine = lax.all_to_all(spread, NEAR, 0, 0).reshape(total, qcount)
    other = lax.ppermute(mine, "c", swap)
    out = local_intensity(place, mine, other, wigner, 2, rows)
    return out + lax.ppermute(out, "deg", swap)


def solution(mesh):
    grid = Mesh(mesh.devices.reshape(4, 2, 4, 2, 2, 2), ("y", "xl", "zh", "zl", "c", "deg"))
    slab = ("y", "xl", "zh", "zl", "c")
    in_specs = (
        P(slab, "deg", None),
        P(slab),
        P(slab),
        P(slab),
        P(),
        P(None, "deg", None),
        P(slab, "deg", None, None),
    )
    return jax.shard_map(
        per_device, mesh=grid, in_specs=in_specs, out_specs=P(slab, None), check_vma=False
    )
```

```python
import functools
import jax
import jax.numpy as jnp
from jax import lax
from jax.experimental import pallas as pl
from jax.experimental.pallas import tpu as pltpu
from jax.sharding import Mesh, PartitionSpec as P

SHELLS = 64
TYPES = 8
BINS = SHELLS * TYPES
NEAR = ("y", "xl", "zl")
FAR = "zh"
PLANE = 16
LIMIT = 8
AMPLITUDE_MIB = 48
TURN_MIB = 16


def widths(local_deg, step):
    return [-(-(2 * (local_deg + j) + 1) // step) * step for j in range(local_deg)]


def starts(rows):
    return [sum(rows[:j]) for j in range(len(rows))]


def coded(x, spare):
    top = jnp.maximum(jnp.max(jnp.abs(x), axis=0, keepdims=True), 1e-30)
    power = jnp.floor(jnp.log2(top)) + 1.0
    steps = jnp.clip(jnp.round(x * jnp.exp2(15.0 - power)), -32767.0, 32767.0)
    tail = jnp.broadcast_to(power, (spare, x.shape[1]))
    return jnp.concatenate([steps, tail], axis=0).astype(jnp.int32).astype(jnp.int16)


def decoded(block, rows):
    wide = block.astype(jnp.int32).astype(jnp.float32)
    return wide[:rows] * jnp.exp2(wide[rows : rows + 1] - 15.0)


def amplitude_kernel(
    scale, rows, thin, place, keys, harmonic, bessel, form, keep, give,
    atoms, waves, forms, onehot, turned, high, low, away, atom_sems, wave_sem, form_sem,
):
    width = harmonic.shape[2]
    qcount = form.shape[1]
    degs = len(rows)
    fetch = [
        pltpu.make_async_copy(harmonic.at[j], atoms.at[j], atom_sems.at[j]) for j in range(degs)
    ]
    for copy in fetch:
        copy.start()
    wave_copy = pltpu.make_async_copy(bessel, waves, wave_sem)
    wave_copy.start()
    form_copy = pltpu.make_async_copy(form, forms, form_sem)
    form_copy.start()

    slots = lax.broadcasted_iota(jnp.int32, (width, 2 * BINS), 1).astype(jnp.float32)
    for i in range(atoms.shape[1] // width):
        line = keys[:, i * width : (i + 1) * width].astype(jnp.float32)
        tall = jnp.transpose(jnp.broadcast_to(line, (width, width)))
        same = slots == jnp.concatenate([tall] * (2 * BINS // width), axis=1)
        onehot[i * width : (i + 1) * width, :] = jnp.where(same, 1.0, 0.0).astype(jnp.bfloat16)
    used = sum(thin)
    blank = jnp.zeros((keep.shape[0] - used, qcount), jnp.float32)
    keep[used:, :] = blank
    away[used:, :] = blank

    wide_at, thin_at = starts(rows), starts(thin)

    def turn(j):
        fetch[j].wait()
        turned[wide_at[j] : wide_at[j] + rows[j], :] = jnp.transpose(atoms[j])[: rows[j]]

    def bin_rows(first, last):
        there = slice(wide_at[first], wide_at[last] + rows[last])
        binned = jnp.dot(turned[there, :], onehot[...], preferred_element_type=jnp.float32)
        top = binned.astype(jnp.bfloat16)
        high[there, :] = top
        low[there, :] = (binned - top.astype(jnp.float32)).astype(jnp.bfloat16)

    def mix(j):
        wide = rows[j]
        radial = (waves[j][:, None, :] * forms[...][None]).reshape(BINS, qcount)
        radial_hi = radial.astype(jnp.bfloat16)
        radial_lo = (radial - radial_hi.astype(jnp.float32)).astype(jnp.bfloat16)
        there = slice(wide_at[j], wide_at[j] + wide)
        tops = [high[there, :BINS], high[there, BINS:]]
        lows = [low[there, :BINS], low[there, BINS:]]
        main = jnp.dot(
            jnp.concatenate(tops + lows, axis=0), radial_hi, preferred_element_type=jnp.float32
        )
        rest = jnp.dot(
            jnp.concatenate(tops, axis=0), radial_lo, preferred_element_type=jnp.float32
        )
        out = (main[: 2 * wide] + (main[2 * wide :] + rest)) * scale
        live = 2 * (place[0] + j) + 1
        order = lax.broadcasted_iota(jnp.int32, (wide, qcount), 0)
        at = slice(thin_at[j], thin_at[j] + thin[j])
        keep[at, :] = jnp.where(order < live, out[:wide], 0.0)[: thin[j]]
        away[at, :] = jnp.where(order < live, out[wide:], 0.0)[: thin[j]]

    cuts = [(0, 5), (6, 13), (14, 21), (22, degs - 1)]
    for j in range(degs):
        turn(j)
    for first, last in cuts:
        bin_rows(first, last)
    wave_copy.wait()
    form_copy.wait()
    for j in range(degs):
        mix(j)
    height = keep.shape[0] // give.shape[0]
    for i in range(give.shape[0]):
        give[i] = coded(away[i * height : (i + 1) * height, :], give.shape[1] - height)


def local_amplitude(place, keys, harmonic, bessel, form, height, scale, rows, thin):
    degs, atoms, width = harmonic.shape
    qcount = form.shape[1]
    live_rows = sum(rows)
    outs = [
        jax.ShapeDtypeStruct((PLANE * height, qcount), jnp.float32),
        jax.ShapeDtypeStruct((PLANE, height + 8, qcount), jnp.int16),
    ]
    return pl.pallas_call(
        functools.partial(amplitude_kernel, scale, rows, thin),
        in_specs=[
            pl.BlockSpec(memory_space=pltpu.SMEM),
            pl.BlockSpec(memory_space=pltpu.VMEM),
            pl.BlockSpec(memory_space=pl.ANY),
            pl.BlockSpec(memory_space=pl.ANY),
            pl.BlockSpec(memory_space=pl.ANY),
        ],
        out_specs=[pl.BlockSpec(memory_space=pltpu.VMEM)] * 2,
        out_shape=outs,
        scratch_shapes=[
            pltpu.VMEM((degs, atoms, width), jnp.bfloat16),
            pltpu.VMEM(bessel.shape, jnp.float32),
            pltpu.VMEM(form.shape, jnp.float32),
            pltpu.VMEM((atoms, 2 * BINS), jnp.bfloat16),
            pltpu.VMEM((live_rows, atoms), jnp.bfloat16),
            pltpu.VMEM((live_rows, 2 * BINS), jnp.bfloat16),
            pltpu.VMEM((live_rows, 2 * BINS), jnp.bfloat16),
            pltpu.VMEM(outs[0].shape, jnp.float32),
            pltpu.SemaphoreType.DMA((degs,)),
            pltpu.SemaphoreType.DMA,
            pltpu.SemaphoreType.DMA,
        ],
        compiler_params=pltpu.CompilerParams(vmem_limit_bytes=AMPLITUDE_MIB * 2**20),
        cost_estimate=pl.CostEstimate(
            flops=2 * live_rows * (2 * BINS * atoms + 6 * BINS * qcount),
            bytes_accessed=harmonic.size * 2 + bessel.size * 4,
            transcendentals=0,
        ),
    )(place, keys, harmonic, bessel, form)


def turn_kernel(rows, thin, place, mine, other, wigner, out, first, second):
    rots, degs, width, _ = wigner.shape
    qcount = mine.shape[1]

    @pl.when(place[1] == 0)
    def _():
        first[...] = mine[...].astype(jnp.float32)
        second[...] = other[...].astype(jnp.float32)

    @pl.when(place[1] != 0)
    def _():
        first[...] = other[...].astype(jnp.float32)
        second[...] = mine[...].astype(jnp.float32)

    acc = [jnp.zeros((8, qcount), jnp.float32)] * rots
    thin_at = starts(thin)
    for j in range(degs):
        wide, some, at = rows[j], thin[j], thin_at[j]
        right = second[at : at + some, :]
        pad = jnp.zeros((width - some, qcount), jnp.float32)
        right = jnp.concatenate([right, pad], axis=0).astype(jnp.bfloat16)
        blocks = jnp.concatenate([wigner[r, j][:wide] for r in range(rots)], axis=0)
        turned = jnp.dot(blocks, right, preferred_element_type=jnp.float32)
        left = first[at : at + some, :]
        for r in range(rots):
            prod = turned[r * wide : r * wide + some] * left
            acc[r] = acc[r] + jnp.sum(prod.reshape(some // 8, 8, qcount), axis=0)
    for r in range(rots):
        out[r : r + 1, :] = jnp.sum(acc[r], axis=0, keepdims=True) * (0.5 / degs)


def local_intensity(place, mine, other, wigner, rows, thin):
    rots = wigner.shape[0]
    total, qcount = mine.shape
    vmem = pl.BlockSpec(memory_space=pltpu.VMEM)
    return pl.pallas_call(
        functools.partial(turn_kernel, rows, thin),
        in_specs=[pl.BlockSpec(memory_space=pltpu.SMEM), vmem, vmem, vmem],
        out_specs=vmem,
        out_shape=jax.ShapeDtypeStruct((rots, qcount), jnp.float32),
        scratch_shapes=[pltpu.VMEM((total, qcount), jnp.float32)] * 2,
        compiler_params=pltpu.CompilerParams(vmem_limit_bytes=TURN_MIB * 2**20),
        cost_estimate=pl.CostEstimate(
            flops=2 * wigner.size * qcount,
            bytes_accessed=wigner.size * 2 + mine.size * 4,
            transcendentals=0,
        ),
    )(place, mine, other, wigner)


def near_kernel(rows, keep, recv, out):
    for i in range(out.shape[0]):
        at = pl.ds(i * rows, rows)
        out[i] = coded(keep[at, :] + decoded(recv[i], rows), out.shape[1] - rows)


def plane_kernel(rows, near, total, code):
    acc = decoded(near[0], rows)
    for i in range(1, near.shape[0]):
        acc = acc + decoded(near[i], rows)
    total[...] = acc
    code[...] = coded(acc, code.shape[0] - rows)


def whole_kernel(total, after, before, across, out):
    rows = total.shape[0]
    acc = total[...] + decoded(across[...], rows)
    acc = acc + (decoded(after[...], rows) + decoded(before[...], rows))
    block = acc.astype(jnp.bfloat16)
    for i in range(out.shape[0]):
        out[i] = block


def whole_call(body, out_shape, limit, *args):
    spec = pl.BlockSpec(memory_space=pltpu.VMEM)
    return pl.pallas_call(
        body,
        in_specs=[spec] * len(args),
        out_specs=jax.tree.map(lambda _: spec, out_shape),
        out_shape=out_shape,
        compiler_params=pltpu.CompilerParams(vmem_limit_bytes=limit * 2**20),
    )(*args)


def per_device(harmonic, shell, atom_type, domain, form, bessel, wigner):
    atom_rows, local_deg, width = harmonic.shape
    qcount = form.shape[1]
    rows, thin = widths(local_deg, 16), widths(local_deg, 8)
    height = -(-sum(thin) // (8 * PLANE)) * 8
    total = height * PLANE
    core = lax.axis_index("c")
    swap = [(0, 1), (1, 0)]
    place = jnp.stack([lax.axis_index("deg") * local_deg, core]).astype(jnp.int32)
    side = jnp.where(core == 0, domain, 1 - domain)
    keys = ((side * SHELLS + shell) * TYPES + atom_type)[None]
    keep, give = local_amplitude(
        place,
        keys,
        harmonic.transpose(1, 0, 2),
        bessel.transpose(1, 0, 2),
        form,
        height,
        (atom_rows * 128) ** -0.5,
        rows,
        thin,
    )
    recv = lax.ppermute(give, "c", swap)
    coded_shape = (height + 8, qcount)
    near = whole_call(
        functools.partial(near_kernel, height),
        jax.ShapeDtypeStruct((PLANE,) + coded_shape, jnp.int16),
        LIMIT,
        keep,
        recv,
    )
    near = lax.all_to_all(near, NEAR, 0, 0)
    part, code = whole_call(
        functools.partial(plane_kernel, height),
        [
            jax.ShapeDtypeStruct((height, qcount), jnp.float32),
            jax.ShapeDtypeStruct(coded_shape, jnp.int16),
        ],
        LIMIT,
        near,
    )
    turns = [lax.ppermute(code, FAR, [(i, (i + k) % 4) for i in range(4)]) for k in (1, 3, 2)]
    spread = whole_call(
        whole_kernel,
        jax.ShapeDtypeStruct((PLANE, height, qcount), jnp.bfloat16),
        LIMIT,
        part,
        *turns,
    )
    mine = lax.all_to_all(spread, NEAR, 0, 0).reshape(total, qcount)
    other = lax.ppermute(mine, "c", swap)
    out = local_intensity(place, mine, other, wigner, rows, thin)
    return out + lax.ppermute(out, "deg", swap)


def solution(mesh):
    grid = Mesh(mesh.devices.reshape(4, 2, 4, 2, 2, 2), ("y", "xl", "zh", "zl", "c", "deg"))
    slab = ("y", "xl", "zh", "zl", "c")
    in_specs = (
        P(slab, "deg", None),
        P(slab),
        P(slab),
        P(slab),
        P(),
        P(None, "deg", None),
        P(slab, "deg", None, None),
    )
    return jax.shard_map(
        per_device, mesh=grid, in_specs=in_specs, out_specs=P(slab, None), check_vma=False
    )
```

```python
import functools
import jax
import jax.numpy as jnp
from jax import lax
from jax.experimental import pallas as pl
from jax.experimental.pallas import tpu as pltpu
from jax.sharding import Mesh, PartitionSpec as P

SHELLS = 64
TYPES = 8
BINS = SHELLS * TYPES
NEAR = ("y", "xl", "zl")
FAR = "zh"
PLANE = 16
LIMIT = 8
AMPLITUDE_MIB = 48
TURN_MIB = 16


def widths(local_deg, step):
    return [-(-(2 * (local_deg + j) + 1) // step) * step for j in range(local_deg)]


def starts(rows):
    return [sum(rows[:j]) for j in range(len(rows))]


def coded(x):
    last = x.shape[0] - 1
    order = lax.broadcasted_iota(jnp.int32, x.shape, 0)
    size = jnp.where(order < last, jnp.abs(x), 0.0)
    top = jnp.maximum(jnp.max(size, axis=0, keepdims=True), 1e-30)
    power = jnp.floor(jnp.log2(top)) + 1.0
    steps = jnp.clip(jnp.round(x * jnp.exp2(15.0 - power)), -32767.0, 32767.0)
    return jnp.where(order < last, steps, power).astype(jnp.int32).astype(jnp.int16)


def decoded(block):
    wide = block.astype(jnp.int32).astype(jnp.float32)
    return wide * jnp.exp2(wide[block.shape[0] - 1 :] - 15.0)


def amplitude_kernel(
    scale, rows, thin, place, keys, harmonic, bessel, form, keep, give,
    atoms, waves, forms, onehot, turned, high, low, away, atom_sems, wave_sem, form_sem,
):
    width = harmonic.shape[2]
    qcount = form.shape[1]
    degs = len(rows)
    fetch = [
        pltpu.make_async_copy(harmonic.at[j], atoms.at[j], atom_sems.at[j]) for j in range(degs)
    ]
    for copy in fetch:
        copy.start()
    wave_copy = pltpu.make_async_copy(bessel, waves, wave_sem)
    wave_copy.start()
    form_copy = pltpu.make_async_copy(form, forms, form_sem)
    form_copy.start()

    slots = lax.broadcasted_iota(jnp.int32, (width, 2 * BINS), 1).astype(jnp.float32)
    for i in range(atoms.shape[1] // width):
        line = keys[:, i * width : (i + 1) * width].astype(jnp.float32)
        tall = jnp.transpose(jnp.broadcast_to(line, (width, width)))
        same = slots == jnp.concatenate([tall] * (2 * BINS // width), axis=1)
        onehot[i * width : (i + 1) * width, :] = jnp.where(same, 1.0, 0.0).astype(jnp.bfloat16)
    used = sum(thin)
    base = used // 8 * 8
    blank = jnp.zeros((keep.shape[0] - base, qcount), jnp.float32)
    keep[base:, :] = blank
    away[base:, :] = blank

    wide_at, thin_at = starts(rows), starts(thin)

    def turn(j):
        fetch[j].wait()
        turned[wide_at[j] : wide_at[j] + rows[j], :] = jnp.transpose(atoms[j])[: rows[j]]

    def bin_rows(first, last):
        there = slice(wide_at[first], wide_at[last] + rows[last])
        binned = jnp.dot(turned[there, :], onehot[...], preferred_element_type=jnp.float32)
        top = binned.astype(jnp.bfloat16)
        high[there, :] = top
        low[there, :] = (binned - top.astype(jnp.float32)).astype(jnp.bfloat16)

    def mix(j):
        wide = rows[j]
        radial = (waves[j][:, None, :] * forms[...][None]).reshape(BINS, qcount)
        radial_hi = radial.astype(jnp.bfloat16)
        radial_lo = (radial - radial_hi.astype(jnp.float32)).astype(jnp.bfloat16)
        there = slice(wide_at[j], wide_at[j] + wide)
        tops = [high[there, :BINS], high[there, BINS:]]
        lows = [low[there, :BINS], low[there, BINS:]]
        main = jnp.dot(
            jnp.concatenate(tops + lows, axis=0), radial_hi, preferred_element_type=jnp.float32
        )
        rest = jnp.dot(
            jnp.concatenate(tops, axis=0), radial_lo, preferred_element_type=jnp.float32
        )
        out = (main[: 2 * wide] + (main[2 * wide :] + rest)) * scale
        live = 2 * (place[0] + j) + 1
        order = lax.broadcasted_iota(jnp.int32, (wide, qcount), 0)
        at = slice(thin_at[j], thin_at[j] + thin[j])
        keep[at, :] = jnp.where(order < live, out[:wide], 0.0)[: thin[j]]
        away[at, :] = jnp.where(order < live, out[wide:], 0.0)[: thin[j]]

    cuts = [(0, 5), (6, 13), (14, 21), (22, degs - 1)]
    for j in range(degs):
        turn(j)
    for first, last in cuts:
        bin_rows(first, last)
    wave_copy.wait()
    form_copy.wait()
    for j in range(degs):
        mix(j)
    height = give.shape[1]
    for i in range(give.shape[0]):
        at = i * (height - 1)
        give[i] = coded(away[at : at + height, :])


def local_amplitude(place, keys, harmonic, bessel, form, height, scale, rows, thin):
    degs, atoms, width = harmonic.shape
    qcount = form.shape[1]
    live_rows = sum(rows)
    outs = [
        jax.ShapeDtypeStruct((PLANE * (height - 1) + 8, qcount), jnp.float32),
        jax.ShapeDtypeStruct((PLANE, height, qcount), jnp.int16),
    ]
    return pl.pallas_call(
        functools.partial(amplitude_kernel, scale, rows, thin),
        in_specs=[
            pl.BlockSpec(memory_space=pltpu.SMEM),
            pl.BlockSpec(memory_space=pltpu.VMEM),
            pl.BlockSpec(memory_space=pl.ANY),
            pl.BlockSpec(memory_space=pl.ANY),
            pl.BlockSpec(memory_space=pl.ANY),
        ],
        out_specs=[pl.BlockSpec(memory_space=pltpu.VMEM)] * 2,
        out_shape=outs,
        scratch_shapes=[
            pltpu.VMEM((degs, atoms, width), jnp.bfloat16),
            pltpu.VMEM(bessel.shape, jnp.float32),
            pltpu.VMEM(form.shape, jnp.float32),
            pltpu.VMEM((atoms, 2 * BINS), jnp.bfloat16),
            pltpu.VMEM((live_rows, atoms), jnp.bfloat16),
            pltpu.VMEM((live_rows, 2 * BINS), jnp.bfloat16),
            pltpu.VMEM((live_rows, 2 * BINS), jnp.bfloat16),
            pltpu.VMEM(outs[0].shape, jnp.float32),
            pltpu.SemaphoreType.DMA((degs,)),
            pltpu.SemaphoreType.DMA,
            pltpu.SemaphoreType.DMA,
        ],
        compiler_params=pltpu.CompilerParams(vmem_limit_bytes=AMPLITUDE_MIB * 2**20),
        cost_estimate=pl.CostEstimate(
            flops=2 * live_rows * (2 * BINS * atoms + 6 * BINS * qcount),
            bytes_accessed=harmonic.size * 2 + bessel.size * 4,
            transcendentals=0,
        ),
    )(place, keys, harmonic, bessel, form)


def turn_kernel(rows, thin, place, mine, other, wigner, out, first, second):
    rots, degs, width, _ = wigner.shape
    qcount = mine.shape[2]

    height = mine.shape[1]

    def unpack(block, into):
        for i in range(block.shape[0]):
            at = i * (height - 1)
            into[at : at + height, :] = block[i].astype(jnp.float32)

    @pl.when(place[1] == 0)
    def _():
        unpack(mine, first)
        unpack(other, second)

    @pl.when(place[1] != 0)
    def _():
        unpack(other, first)
        unpack(mine, second)

    order = lax.broadcasted_iota(jnp.int32, (width, qcount), 0)
    acc = [jnp.zeros((8, qcount), jnp.float32)] * rots
    thin_at = starts(thin)
    for j in range(degs):
        wide, some, at = rows[j], thin[j], thin_at[j]
        right = jnp.where(order < some, second[at : at + width, :], 0.0).astype(jnp.bfloat16)
        blocks = jnp.concatenate([wigner[r, j][:wide] for r in range(rots)], axis=0)
        turned = jnp.dot(blocks, right, preferred_element_type=jnp.float32)
        left = jnp.where(order[:wide] < some, first[at : at + wide, :], 0.0)
        for r in range(rots):
            prod = turned[r * wide : (r + 1) * wide] * left
            acc[r] = acc[r] + jnp.sum(prod.reshape(wide // 8, 8, qcount), axis=0)
    for r in range(rots):
        out[r : r + 1, :] = jnp.sum(acc[r], axis=0, keepdims=True) * (0.5 / degs)


def local_intensity(place, mine, other, wigner, rows, thin):
    rots = wigner.shape[0]
    parts, height, qcount = mine.shape
    total = -(-(parts * (height - 1) + wigner.shape[2]) // 8) * 8
    vmem = pl.BlockSpec(memory_space=pltpu.VMEM)
    return pl.pallas_call(
        functools.partial(turn_kernel, rows, thin),
        in_specs=[pl.BlockSpec(memory_space=pltpu.SMEM), vmem, vmem, vmem],
        out_specs=vmem,
        out_shape=jax.ShapeDtypeStruct((rots, qcount), jnp.float32),
        scratch_shapes=[pltpu.VMEM((total, qcount), jnp.float32)] * 2,
        compiler_params=pltpu.CompilerParams(vmem_limit_bytes=TURN_MIB * 2**20),
        cost_estimate=pl.CostEstimate(
            flops=2 * wigner.size * qcount,
            bytes_accessed=wigner.size * 2 + mine.size * 4,
            transcendentals=0,
        ),
    )(place, mine, other, wigner)


def near_kernel(keep, recv, out):
    height = out.shape[1]
    for i in range(out.shape[0]):
        at = i * (height - 1)
        out[i] = coded(keep[at : at + height, :] + decoded(recv[i]))


def plane_kernel(near, total, code):
    acc = decoded(near[0])
    for i in range(1, near.shape[0]):
        acc = acc + decoded(near[i])
    total[...] = acc
    code[...] = coded(acc)


def whole_kernel(total, after, before, across, out):
    acc = total[...] + decoded(across[...])
    acc = acc + (decoded(after[...]) + decoded(before[...]))
    block = acc.astype(jnp.bfloat16)
    for i in range(out.shape[0]):
        out[i] = block


def whole_call(body, out_shape, limit, *args):
    spec = pl.BlockSpec(memory_space=pltpu.VMEM)
    return pl.pallas_call(
        body,
        in_specs=[spec] * len(args),
        out_specs=jax.tree.map(lambda _: spec, out_shape),
        out_shape=out_shape,
        compiler_params=pltpu.CompilerParams(vmem_limit_bytes=limit * 2**20),
    )(*args)


def per_device(harmonic, shell, atom_type, domain, form, bessel, wigner):
    atom_rows, local_deg, width = harmonic.shape
    qcount = form.shape[1]
    rows, thin = widths(local_deg, 16), widths(local_deg, 1)
    height = -(-sum(thin) // PLANE) + 1
    core = lax.axis_index("c")
    swap = [(0, 1), (1, 0)]
    place = jnp.stack([lax.axis_index("deg") * local_deg, core]).astype(jnp.int32)
    side = jnp.where(core == 0, domain, 1 - domain)
    keys = ((side * SHELLS + shell) * TYPES + atom_type)[None]
    keep, give = local_amplitude(
        place,
        keys,
        harmonic.transpose(1, 0, 2),
        bessel.transpose(1, 0, 2),
        form,
        height,
        (atom_rows * 128) ** -0.5,
        rows,
        thin,
    )
    recv = lax.ppermute(give, "c", swap)
    coded_shape = (height, qcount)
    near = whole_call(
        near_kernel,
        jax.ShapeDtypeStruct((PLANE,) + coded_shape, jnp.int16),
        LIMIT,
        keep,
        recv,
    )
    near = lax.all_to_all(near, NEAR, 0, 0)
    part, code = whole_call(
        plane_kernel,
        [
            jax.ShapeDtypeStruct((height, qcount), jnp.float32),
            jax.ShapeDtypeStruct(coded_shape, jnp.int16),
        ],
        LIMIT,
        near,
    )
    turns = [lax.ppermute(code, FAR, [(i, (i + k) % 4) for i in range(4)]) for k in (1, 3, 2)]
    spread = whole_call(
        whole_kernel,
        jax.ShapeDtypeStruct((PLANE, height, qcount), jnp.bfloat16),
        LIMIT,
        part,
        *turns,
    )
    mine = lax.all_to_all(spread, NEAR, 0, 0)
    other = lax.ppermute(mine, "c", swap)
    out = local_intensity(place, mine, other, wigner, rows, thin)
    return out + lax.ppermute(out, "deg", swap)


def solution(mesh):
    grid = Mesh(mesh.devices.reshape(4, 2, 4, 2, 2, 2), ("y", "xl", "zh", "zl", "c", "deg"))
    slab = ("y", "xl", "zh", "zl", "c")
    in_specs = (
        P(slab, "deg", None),
        P(slab),
        P(slab),
        P(slab),
        P(),
        P(None, "deg", None),
        P(slab, "deg", None, None),
    )
    return jax.shard_map(
        per_device, mesh=grid, in_specs=in_specs, out_specs=P(slab, None), check_vma=False
    )
```

```python
import functools
import jax
import jax.numpy as jnp
from jax import lax
from jax.experimental import pallas as pl
from jax.experimental.pallas import tpu as pltpu
from jax.sharding import Mesh, PartitionSpec as P

SHELLS = 64
TYPES = 8
BINS = SHELLS * TYPES
NEAR = ("y", "xl", "zl")
FAR = "zh"
PLANE = 16
LIMIT = 8
AMPLITUDE_MIB = 48
TURN_MIB = 16


def widths(local_deg, step):
    return [-(-(2 * (local_deg + j) + 1) // step) * step for j in range(local_deg)]


def starts(rows):
    return [sum(rows[:j]) for j in range(len(rows))]


def coded(x):
    last = x.shape[0] - 1
    order = lax.broadcasted_iota(jnp.int32, x.shape, 0)
    size = jnp.where(order < last, jnp.abs(x), 0.0)
    top = jnp.maximum(jnp.max(size, axis=0, keepdims=True), 1e-30)
    power = jnp.floor(jnp.log2(top)) + 1.0
    steps = jnp.clip(jnp.round(x * jnp.exp2(15.0 - power)), -32767.0, 32767.0)
    return jnp.where(order < last, steps, power).astype(jnp.int32).astype(jnp.int16)


def decoded(block):
    wide = block.astype(jnp.int32).astype(jnp.float32)
    return wide * jnp.exp2(wide[block.shape[0] - 1 :] - 15.0)


def amplitude_kernel(
    scale, rows, thin, place, keys, harmonic, bessel, form, keep, give,
    atoms, waves, forms, onehot, turned, high, low, away, atom_sems, wave_sem, form_sem,
):
    width = harmonic.shape[2]
    qcount = form.shape[1]
    degs = len(rows)
    fetch = [
        pltpu.make_async_copy(harmonic.at[j], atoms.at[j], atom_sems.at[j]) for j in range(degs)
    ]
    for copy in fetch:
        copy.start()
    wave_copy = pltpu.make_async_copy(bessel, waves, wave_sem)
    wave_copy.start()
    form_copy = pltpu.make_async_copy(form, forms, form_sem)
    form_copy.start()

    slots = lax.broadcasted_iota(jnp.int32, (width, 2 * BINS), 1).astype(jnp.float32)
    for i in range(atoms.shape[1] // width):
        line = keys[:, i * width : (i + 1) * width].astype(jnp.float32)
        tall = jnp.transpose(jnp.broadcast_to(line, (width, width)))
        same = slots == jnp.concatenate([tall] * (2 * BINS // width), axis=1)
        onehot[i * width : (i + 1) * width, :] = jnp.where(same, 1.0, 0.0).astype(jnp.bfloat16)
    height = give.shape[1]
    blank = jnp.zeros((8, qcount), jnp.float32)
    keep[keep.shape[0] - 8 :, :] = blank
    away[keep.shape[0] - 8 :, :] = blank

    wide_at, thin_at = starts(rows), starts(thin)

    def turn(j):
        turned[wide_at[j] : wide_at[j] + rows[j], :] = jnp.transpose(atoms[j])[: rows[j]]

    def bin_rows(first, last):
        there = slice(wide_at[first], wide_at[last] + rows[last])
        binned = jnp.dot(turned[there, :], onehot[...], preferred_element_type=jnp.float32)
        top = binned.astype(jnp.bfloat16)
        high[there, :] = top
        low[there, :] = (binned - top.astype(jnp.float32)).astype(jnp.bfloat16)

    def mix(j):
        wide = rows[j]
        radial = (waves[j][:, None, :] * forms[...][None]).reshape(BINS, qcount)
        radial_hi = radial.astype(jnp.bfloat16)
        radial_lo = (radial - radial_hi.astype(jnp.float32)).astype(jnp.bfloat16)
        there = slice(wide_at[j], wide_at[j] + wide)
        tops = [high[there, :BINS], high[there, BINS:]]
        lows = [low[there, :BINS], low[there, BINS:]]
        main = jnp.dot(
            jnp.concatenate(tops + lows, axis=0), radial_hi, preferred_element_type=jnp.float32
        )
        rest = jnp.dot(
            jnp.concatenate(tops, axis=0), radial_lo, preferred_element_type=jnp.float32
        )
        out = (main[: 2 * wide] + (main[2 * wide :] + rest)) * scale
        live = 2 * (place[0] + j) + 1
        order = lax.broadcasted_iota(jnp.int32, (wide, qcount), 0)
        mine = jnp.where(order < live, out[:wide], 0.0)
        other = jnp.where(order < live, out[wide:], 0.0)
        done = 0
        while done < thin[j]:
            part, row = divmod(thin_at[j] + done, height - 1)
            count = min(thin[j] - done, height - 1 - row)
            at = slice(part * height + row, part * height + row + count)
            keep[at, :] = mine[done : done + count]
            away[at, :] = other[done : done + count]
            done += count

    cuts = [(0, 5), (6, 13), (14, 21), (22, degs - 1)]
    for copy in fetch + [wave_copy, form_copy]:
        copy.wait()
    for j in range(degs):
        turn(j)
    for first, last in cuts:
        bin_rows(first, last)
    for j in range(degs):
        mix(j)
    for i in range(give.shape[0]):
        give[i] = coded(away[i * height : (i + 1) * height, :])


def local_amplitude(place, keys, harmonic, bessel, form, height, scale, rows, thin):
    degs, atoms, width = harmonic.shape
    qcount = form.shape[1]
    live_rows = sum(rows)
    outs = [
        jax.ShapeDtypeStruct((PLANE * height, qcount), jnp.float32),
        jax.ShapeDtypeStruct((PLANE, height, qcount), jnp.int16),
    ]
    return pl.pallas_call(
        functools.partial(amplitude_kernel, scale, rows, thin),
        in_specs=[
            pl.BlockSpec(memory_space=pltpu.SMEM),
            pl.BlockSpec(memory_space=pltpu.VMEM),
            pl.BlockSpec(memory_space=pl.ANY),
            pl.BlockSpec(memory_space=pl.ANY),
            pl.BlockSpec(memory_space=pl.ANY),
        ],
        out_specs=[pl.BlockSpec(memory_space=pltpu.VMEM)] * 2,
        out_shape=outs,
        scratch_shapes=[
            pltpu.VMEM((degs, atoms, width), jnp.bfloat16),
            pltpu.VMEM(bessel.shape, jnp.float32),
            pltpu.VMEM(form.shape, jnp.float32),
            pltpu.VMEM((atoms, 2 * BINS), jnp.bfloat16),
            pltpu.VMEM((live_rows, atoms), jnp.bfloat16),
            pltpu.VMEM((live_rows, 2 * BINS), jnp.bfloat16),
            pltpu.VMEM((live_rows, 2 * BINS), jnp.bfloat16),
            pltpu.VMEM(outs[0].shape, jnp.float32),
            pltpu.SemaphoreType.DMA((degs,)),
            pltpu.SemaphoreType.DMA,
            pltpu.SemaphoreType.DMA,
        ],
        compiler_params=pltpu.CompilerParams(vmem_limit_bytes=AMPLITUDE_MIB * 2**20),
        cost_estimate=pl.CostEstimate(
            flops=2 * live_rows * (2 * BINS * atoms + 6 * BINS * qcount),
            bytes_accessed=harmonic.size * 2 + bessel.size * 4,
            transcendentals=0,
        ),
    )(place, keys, harmonic, bessel, form)


def turn_kernel(rows, thin, place, mine, other, wigner, out, first, second):
    rots, degs, width, _ = wigner.shape
    qcount = mine.shape[2]

    height = mine.shape[1]

    def unpack(block, into):
        for i in range(block.shape[0]):
            at = i * (height - 1)
            into[at : at + height, :] = block[i].astype(jnp.float32)

    @pl.when(place[1] == 0)
    def _():
        unpack(mine, first)
        unpack(other, second)

    @pl.when(place[1] != 0)
    def _():
        unpack(other, first)
        unpack(mine, second)

    order = lax.broadcasted_iota(jnp.int32, (width, qcount), 0)
    acc = [jnp.zeros((8, qcount), jnp.float32)] * rots
    thin_at = starts(thin)
    for j in range(degs):
        wide, some, at = rows[j], thin[j], thin_at[j]
        right = jnp.where(order < some, second[at : at + width, :], 0.0).astype(jnp.bfloat16)
        blocks = jnp.concatenate([wigner[r, j][:wide] for r in range(rots)], axis=0)
        turned = jnp.dot(blocks, right, preferred_element_type=jnp.float32)
        left = jnp.where(order[:wide] < some, first[at : at + wide, :], 0.0)
        for r in range(rots):
            prod = turned[r * wide : (r + 1) * wide] * left
            acc[r] = acc[r] + jnp.sum(prod.reshape(wide // 8, 8, qcount), axis=0)
    for r in range(rots):
        out[r : r + 1, :] = jnp.sum(acc[r], axis=0, keepdims=True) * (0.5 / degs)


def local_intensity(place, mine, other, wigner, rows, thin):
    rots = wigner.shape[0]
    parts, height, qcount = mine.shape
    total = -(-(parts * (height - 1) + wigner.shape[2]) // 8) * 8
    vmem = pl.BlockSpec(memory_space=pltpu.VMEM)
    return pl.pallas_call(
        functools.partial(turn_kernel, rows, thin),
        in_specs=[pl.BlockSpec(memory_space=pltpu.SMEM), vmem, vmem, vmem],
        out_specs=vmem,
        out_shape=jax.ShapeDtypeStruct((rots, qcount), jnp.float32),
        scratch_shapes=[pltpu.VMEM((total, qcount), jnp.float32)] * 2,
        compiler_params=pltpu.CompilerParams(vmem_limit_bytes=TURN_MIB * 2**20),
        cost_estimate=pl.CostEstimate(
            flops=2 * wigner.size * qcount,
            bytes_accessed=wigner.size * 2 + mine.size * 4,
            transcendentals=0,
        ),
    )(place, mine, other, wigner)


def near_kernel(keep, recv, out):
    height = out.shape[1]
    for i in range(out.shape[0]):
        out[i] = coded(keep[i * height : (i + 1) * height, :] + decoded(recv[i]))


def plane_kernel(near, total, code):
    acc = decoded(near[0])
    for i in range(1, near.shape[0]):
        acc = acc + decoded(near[i])
    total[...] = acc
    code[...] = coded(acc)


def whole_kernel(total, after, before, across, out):
    acc = total[...] + decoded(across[...])
    acc = acc + (decoded(after[...]) + decoded(before[...]))
    block = acc.astype(jnp.bfloat16)
    for i in range(out.shape[0]):
        out[i] = block


def whole_call(body, out_shape, limit, *args):
    spec = pl.BlockSpec(memory_space=pltpu.VMEM)
    return pl.pallas_call(
        body,
        in_specs=[spec] * len(args),
        out_specs=jax.tree.map(lambda _: spec, out_shape),
        out_shape=out_shape,
        compiler_params=pltpu.CompilerParams(vmem_limit_bytes=limit * 2**20),
    )(*args)


def per_device(harmonic, shell, atom_type, domain, form, bessel, wigner):
    atom_rows, local_deg, width = harmonic.shape
    qcount = form.shape[1]
    rows, thin = widths(local_deg, 16), widths(local_deg, 1)
    height = -(-sum(thin) // PLANE) + 1
    core = lax.axis_index("c")
    swap = [(0, 1), (1, 0)]
    place = jnp.stack([lax.axis_index("deg") * local_deg, core]).astype(jnp.int32)
    side = jnp.where(core == 0, domain, 1 - domain)
    keys = ((side * SHELLS + shell) * TYPES + atom_type)[None]
    keep, give = local_amplitude(
        place,
        keys,
        harmonic.transpose(1, 0, 2),
        bessel.transpose(1, 0, 2),
        form,
        height,
        (atom_rows * 128) ** -0.5,
        rows,
        thin,
    )
    recv = lax.ppermute(give, "c", swap)
    coded_shape = (height, qcount)
    near = whole_call(
        near_kernel,
        jax.ShapeDtypeStruct((PLANE,) + coded_shape, jnp.int16),
        LIMIT,
        keep,
        recv,
    )
    near = lax.all_to_all(near, NEAR, 0, 0)
    part, code = whole_call(
        plane_kernel,
        [
            jax.ShapeDtypeStruct((height, qcount), jnp.float32),
            jax.ShapeDtypeStruct(coded_shape, jnp.int16),
        ],
        LIMIT,
        near,
    )
    turns = [lax.ppermute(code, FAR, [(i, (i + k) % 4) for i in range(4)]) for k in (1, 3, 2)]
    spread = whole_call(
        whole_kernel,
        jax.ShapeDtypeStruct((PLANE, height, qcount), jnp.bfloat16),
        LIMIT,
        part,
        *turns,
    )
    mine = lax.all_to_all(spread, NEAR, 0, 0)
    other = lax.ppermute(mine, "c", swap)
    out = local_intensity(place, mine, other, wigner, rows, thin)
    return out + lax.ppermute(out, "deg", swap)


def solution(mesh):
    grid = Mesh(mesh.devices.reshape(4, 2, 4, 2, 2, 2), ("y", "xl", "zh", "zl", "c", "deg"))
    slab = ("y", "xl", "zh", "zl", "c")
    in_specs = (
        P(slab, "deg", None),
        P(slab),
        P(slab),
        P(slab),
        P(),
        P(None, "deg", None),
        P(slab, "deg", None, None),
    )
    return jax.shard_map(
        per_device, mesh=grid, in_specs=in_specs, out_specs=P(slab, None), check_vma=False
    )
```

```python
import functools
import jax
import jax.numpy as jnp
from jax import lax
from jax.experimental import pallas as pl
from jax.experimental.pallas import tpu as pltpu
from jax.sharding import Mesh, PartitionSpec as P

SHELLS = 64
TYPES = 8
BINS = SHELLS * TYPES
NEAR = ("y", "xl", "zl")
FAR = "zh"
PLANE = 16
LIMIT = 8
AMPLITUDE_MIB = 48
TURN_MIB = 16


def widths(local_deg, step):
    return [-(-(2 * (local_deg + j) + 1) // step) * step for j in range(local_deg)]


def starts(rows):
    return [sum(rows[:j]) for j in range(len(rows))]


def coded(x):
    last = x.shape[0] - 1
    order = lax.broadcasted_iota(jnp.int32, x.shape, 0)
    size = jnp.where(order < last, jnp.abs(x), 0.0)
    top = jnp.maximum(jnp.max(size, axis=0, keepdims=True), 1e-30)
    power = jnp.floor(jnp.log2(top)) + 1.0
    steps = jnp.clip(jnp.round(x * jnp.exp2(15.0 - power)), -32767.0, 32767.0)
    return jnp.where(order < last, steps, power).astype(jnp.int32).astype(jnp.int16)


def decoded(block):
    wide = block.astype(jnp.int32).astype(jnp.float32)
    return wide * jnp.exp2(wide[block.shape[0] - 1 :] - 15.0)


def amplitude_kernel(
    scale, rows, thin, place, keys, harmonic, bessel, form, keep, give,
    atoms, waves, forms, onehot, turned, high, low, away, atom_sems, wave_sem, form_sem,
):
    width = harmonic.shape[2]
    qcount = form.shape[1]
    degs = len(rows)
    fetch = [
        pltpu.make_async_copy(harmonic.at[j], atoms.at[j], atom_sems.at[j]) for j in range(degs)
    ]
    for copy in fetch:
        copy.start()
    wave_copy = pltpu.make_async_copy(bessel, waves, wave_sem)
    wave_copy.start()
    form_copy = pltpu.make_async_copy(form, forms, form_sem)
    form_copy.start()

    slots = lax.broadcasted_iota(jnp.int32, (width, 2 * BINS), 1).astype(jnp.float32)
    for i in range(atoms.shape[1] // width):
        line = keys[:, i * width : (i + 1) * width].astype(jnp.float32)
        tall = jnp.transpose(jnp.broadcast_to(line, (width, width)))
        same = slots == jnp.concatenate([tall] * (2 * BINS // width), axis=1)
        onehot[i * width : (i + 1) * width, :] = jnp.where(same, 1.0, 0.0).astype(jnp.bfloat16)
    height = give.shape[1]
    blank = jnp.zeros((8, qcount), jnp.float32)
    keep[keep.shape[0] - 8 :, :] = blank
    away[keep.shape[0] - 8 :, :] = blank

    wide_at, thin_at = starts(rows), starts(thin)

    def turn(j):
        turned[wide_at[j] : wide_at[j] + rows[j], :] = jnp.transpose(atoms[j])[: rows[j]]

    def bin_rows(first, last):
        there = slice(wide_at[first], wide_at[last] + rows[last])
        binned = jnp.dot(turned[there, :], onehot[...], preferred_element_type=jnp.float32)
        top = binned.astype(jnp.bfloat16)
        high[there, :] = top
        low[there, :] = (binned - top.astype(jnp.float32)).astype(jnp.bfloat16)

    def mix(j):
        wide = rows[j]
        radial = (waves[j][:, None, :] * scaled[None]).reshape(BINS, qcount)
        radial_hi = radial.astype(jnp.bfloat16)
        radial_lo = (radial - radial_hi.astype(jnp.float32)).astype(jnp.bfloat16)
        there = slice(wide_at[j], wide_at[j] + wide)
        tops = [high[there, :BINS], high[there, BINS:]]
        lows = [low[there, :BINS], low[there, BINS:]]
        main = jnp.dot(
            jnp.concatenate(tops + lows, axis=0), radial_hi, preferred_element_type=jnp.float32
        )
        rest = jnp.dot(
            jnp.concatenate(tops, axis=0), radial_lo, preferred_element_type=jnp.float32
        )
        out = (main[: 2 * wide] + (main[2 * wide :] + rest))
        live = 2 * (place[0] + j) + 1
        order = lax.broadcasted_iota(jnp.int32, (wide, qcount), 0)
        mine = jnp.where(order < live, out[:wide], 0.0)
        other = jnp.where(order < live, out[wide:], 0.0)
        done = 0
        while done < thin[j]:
            part, row = divmod(thin_at[j] + done, height - 1)
            count = min(thin[j] - done, height - 1 - row)
            at = slice(part * height + row, part * height + row + count)
            keep[at, :] = mine[done : done + count]
            away[at, :] = other[done : done + count]
            done += count

    cuts = [(0, 5), (6, 13), (14, 21), (22, degs - 1)]
    for first, last in cuts:
        for copy in fetch[first : last + 1]:
            copy.wait()
        for j in range(first, last + 1):
            turn(j)
        bin_rows(first, last)
    wave_copy.wait()
    form_copy.wait()
    scaled = forms[...] * scale
    for j in range(degs):
        mix(j)
    for i in range(give.shape[0]):
        give[i] = coded(away[i * height : (i + 1) * height, :])


def local_amplitude(place, keys, harmonic, bessel, form, height, scale, rows, thin):
    degs, atoms, width = harmonic.shape
    qcount = form.shape[1]
    live_rows = sum(rows)
    outs = [
        jax.ShapeDtypeStruct((PLANE * height, qcount), jnp.float32),
        jax.ShapeDtypeStruct((PLANE, height, qcount), jnp.int16),
    ]
    return pl.pallas_call(
        functools.partial(amplitude_kernel, scale, rows, thin),
        in_specs=[
            pl.BlockSpec(memory_space=pltpu.SMEM),
            pl.BlockSpec(memory_space=pltpu.VMEM),
            pl.BlockSpec(memory_space=pl.ANY),
            pl.BlockSpec(memory_space=pl.ANY),
            pl.BlockSpec(memory_space=pl.ANY),
        ],
        out_specs=[pl.BlockSpec(memory_space=pltpu.VMEM)] * 2,
        out_shape=outs,
        scratch_shapes=[
            pltpu.VMEM((degs, atoms, width), jnp.bfloat16),
            pltpu.VMEM(bessel.shape, jnp.float32),
            pltpu.VMEM(form.shape, jnp.float32),
            pltpu.VMEM((atoms, 2 * BINS), jnp.bfloat16),
            pltpu.VMEM((live_rows, atoms), jnp.bfloat16),
            pltpu.VMEM((live_rows, 2 * BINS), jnp.bfloat16),
            pltpu.VMEM((live_rows, 2 * BINS), jnp.bfloat16),
            pltpu.VMEM(outs[0].shape, jnp.float32),
            pltpu.SemaphoreType.DMA((degs,)),
            pltpu.SemaphoreType.DMA,
            pltpu.SemaphoreType.DMA,
        ],
        compiler_params=pltpu.CompilerParams(vmem_limit_bytes=AMPLITUDE_MIB * 2**20),
        cost_estimate=pl.CostEstimate(
            flops=2 * live_rows * (2 * BINS * atoms + 6 * BINS * qcount),
            bytes_accessed=harmonic.size * 2 + bessel.size * 4,
            transcendentals=0,
        ),
    )(place, keys, harmonic, bessel, form)


def turn_kernel(rows, thin, place, mine, other, wigner, out, first, second):
    rots, degs, width, _ = wigner.shape
    qcount = mine.shape[2]

    height = mine.shape[1]

    def unpack(block, into):
        for i in range(block.shape[0]):
            at = i * (height - 1)
            into[at : at + height, :] = block[i].astype(jnp.float32)

    @pl.when(place[1] == 0)
    def _():
        unpack(mine, first)
        unpack(other, second)

    @pl.when(place[1] != 0)
    def _():
        unpack(other, first)
        unpack(mine, second)

    order = lax.broadcasted_iota(jnp.int32, (width, qcount), 0)
    acc = [jnp.zeros((8, qcount), jnp.float32)] * rots
    thin_at = starts(thin)
    for j in range(degs):
        wide, some, at = rows[j], thin[j], thin_at[j]
        right = jnp.where(order < some, second[at : at + width, :], 0.0).astype(jnp.bfloat16)
        blocks = jnp.concatenate([wigner[r, j][:wide] for r in range(rots)], axis=0)
        turned = jnp.dot(blocks, right, preferred_element_type=jnp.float32)
        left = jnp.where(order[:wide] < some, first[at : at + wide, :], 0.0)
        for r in range(rots):
            prod = turned[r * wide : (r + 1) * wide] * left
            acc[r] = acc[r] + jnp.sum(prod.reshape(wide // 8, 8, qcount), axis=0)
    for r in range(rots):
        out[r : r + 1, :] = jnp.sum(acc[r], axis=0, keepdims=True) * (0.5 / degs)


def local_intensity(place, mine, other, wigner, rows, thin):
    rots = wigner.shape[0]
    parts, height, qcount = mine.shape
    total = -(-(parts * (height - 1) + wigner.shape[2]) // 8) * 8
    vmem = pl.BlockSpec(memory_space=pltpu.VMEM)
    return pl.pallas_call(
        functools.partial(turn_kernel, rows, thin),
        in_specs=[pl.BlockSpec(memory_space=pltpu.SMEM), vmem, vmem, vmem],
        out_specs=vmem,
        out_shape=jax.ShapeDtypeStruct((rots, qcount), jnp.float32),
        scratch_shapes=[pltpu.VMEM((total, qcount), jnp.float32)] * 2,
        compiler_params=pltpu.CompilerParams(vmem_limit_bytes=TURN_MIB * 2**20),
        cost_estimate=pl.CostEstimate(
            flops=2 * wigner.size * qcount,
            bytes_accessed=wigner.size * 2 + mine.size * 4,
            transcendentals=0,
        ),
    )(place, mine, other, wigner)


def near_kernel(keep, recv, out):
    height = out.shape[1]
    for i in range(out.shape[0]):
        out[i] = coded(keep[i * height : (i + 1) * height, :] + decoded(recv[i]))


def plane_kernel(near, total, code):
    acc = decoded(near[0])
    for i in range(1, near.shape[0]):
        acc = acc + decoded(near[i])
    total[...] = acc
    code[...] = coded(acc)


def whole_kernel(total, after, before, across, out):
    acc = total[...] + decoded(across[...])
    acc = acc + (decoded(after[...]) + decoded(before[...]))
    block = acc.astype(jnp.bfloat16)
    for i in range(out.shape[0]):
        out[i] = block


def whole_call(body, out_shape, limit, *args):
    spec = pl.BlockSpec(memory_space=pltpu.VMEM)
    return pl.pallas_call(
        body,
        in_specs=[spec] * len(args),
        out_specs=jax.tree.map(lambda _: spec, out_shape),
        out_shape=out_shape,
        compiler_params=pltpu.CompilerParams(vmem_limit_bytes=limit * 2**20),
    )(*args)


def per_device(harmonic, shell, atom_type, domain, form, bessel, wigner):
    atom_rows, local_deg, width = harmonic.shape
    qcount = form.shape[1]
    rows, thin = widths(local_deg, 16), widths(local_deg, 1)
    height = -(-sum(thin) // PLANE) + 1
    core = lax.axis_index("c")
    swap = [(0, 1), (1, 0)]
    place = jnp.stack([lax.axis_index("deg") * local_deg, core]).astype(jnp.int32)
    side = jnp.where(core == 0, domain, 1 - domain)
    keys = ((side * SHELLS + shell) * TYPES + atom_type)[None]
    keep, give = local_amplitude(
        place,
        keys,
        harmonic.transpose(1, 0, 2),
        bessel.transpose(1, 0, 2),
        form,
        height,
        (atom_rows * 128) ** -0.5,
        rows,
        thin,
    )
    recv = lax.ppermute(give, "c", swap)
    coded_shape = (height, qcount)
    near = whole_call(
        near_kernel,
        jax.ShapeDtypeStruct((PLANE,) + coded_shape, jnp.int16),
        LIMIT,
        keep,
        recv,
    )
    near = lax.all_to_all(near, NEAR, 0, 0)
    part, code = whole_call(
        plane_kernel,
        [
            jax.ShapeDtypeStruct((height, qcount), jnp.float32),
            jax.ShapeDtypeStruct(coded_shape, jnp.int16),
        ],
        LIMIT,
        near,
    )
    turns = [lax.ppermute(code, FAR, [(i, (i + k) % 4) for i in range(4)]) for k in (1, 3, 2)]
    spread = whole_call(
        whole_kernel,
        jax.ShapeDtypeStruct((PLANE, height, qcount), jnp.bfloat16),
        LIMIT,
        part,
        *turns,
    )
    mine = lax.all_to_all(spread, NEAR, 0, 0)
    other = lax.ppermute(mine, "c", swap)
    out = local_intensity(place, mine, other, wigner, rows, thin)
    return out + lax.ppermute(out, "deg", swap)


def solution(mesh):
    grid = Mesh(mesh.devices.reshape(4, 2, 4, 2, 2, 2), ("y", "xl", "zh", "zl", "c", "deg"))
    slab = ("y", "xl", "zh", "zl", "c")
    in_specs = (
        P(slab, "deg", None),
        P(slab),
        P(slab),
        P(slab),
        P(),
        P(None, "deg", None),
        P(slab, "deg", None, None),
    )
    return jax.shard_map(
        per_device, mesh=grid, in_specs=in_specs, out_specs=P(slab, None), check_vma=False
    )
```

```python
import functools
import jax
import jax.numpy as jnp
from jax import lax
from jax.experimental import pallas as pl
from jax.experimental.pallas import tpu as pltpu
from jax.sharding import Mesh, PartitionSpec as P

SHELLS = 64
TYPES = 8
BINS = SHELLS * TYPES
NEAR = ("y", "xl", "zl")
FAR = "zh"
PLANE = 16
LIMIT = 8
AMPLITUDE_MIB = 48
TURN_MIB = 16


def widths(local_deg, step):
    return [-(-(2 * (local_deg + j) + 1) // step) * step for j in range(local_deg)]


def starts(rows):
    return [sum(rows[:j]) for j in range(len(rows))]


def coded(x):
    last = x.shape[0] - 1
    order = lax.broadcasted_iota(jnp.int32, x.shape, 0)
    size = jnp.where(order < last, jnp.abs(x), 0.0)
    top = jnp.maximum(jnp.max(size, axis=0, keepdims=True), 1e-30)
    power = jnp.floor(jnp.log2(top)) + 1.0
    steps = jnp.clip(jnp.round(x * jnp.exp2(15.0 - power)), -32767.0, 32767.0)
    return jnp.where(order < last, steps, power).astype(jnp.int32).astype(jnp.int16)


def decoded(block):
    wide = block.astype(jnp.int32).astype(jnp.float32)
    return wide * jnp.exp2(wide[block.shape[0] - 1 :] - 15.0)


def amplitude_kernel(
    scale, rows, thin, place, keys, harmonic, bessel, form, keep, give,
    atoms, waves, forms, onehot, turned, high, low, away, atom_sems, wave_sem, form_sem,
):
    width = harmonic.shape[2]
    qcount = form.shape[1]
    degs = len(rows)
    fetch = [
        pltpu.make_async_copy(harmonic.at[j], atoms.at[j], atom_sems.at[j]) for j in range(degs)
    ]
    for copy in fetch:
        copy.start()
    wave_copy = pltpu.make_async_copy(bessel, waves, wave_sem)
    wave_copy.start()
    form_copy = pltpu.make_async_copy(form, forms, form_sem)
    form_copy.start()

    slots = lax.broadcasted_iota(jnp.int32, (width, 2 * BINS), 1).astype(jnp.float32)
    for i in range(atoms.shape[1] // width):
        line = keys[:, i * width : (i + 1) * width].astype(jnp.float32)
        tall = jnp.transpose(jnp.broadcast_to(line, (width, width)))
        same = slots == jnp.concatenate([tall] * (2 * BINS // width), axis=1)
        onehot[i * width : (i + 1) * width, :] = jnp.where(same, 1.0, 0.0).astype(jnp.bfloat16)
    height = give.shape[1]
    blank = jnp.zeros((8, qcount), jnp.float32)
    keep[keep.shape[0] - 8 :, :] = blank
    away[keep.shape[0] - 8 :, :] = blank

    wide_at, thin_at = starts(rows), starts(thin)

    def turn(j):
        turned[wide_at[j] : wide_at[j] + rows[j], :] = jnp.transpose(atoms[j])[: rows[j]]

    def bin_rows(first, last):
        there = slice(wide_at[first], wide_at[last] + rows[last])
        binned = jnp.dot(turned[there, :], onehot[...], preferred_element_type=jnp.float32)
        top = binned.astype(jnp.bfloat16)
        high[there, :] = top
        low[there, :] = (binned - top.astype(jnp.float32)).astype(jnp.bfloat16)

    def mix(j):
        wide = rows[j]
        radial = (waves[j][:, None, :] * scaled[None]).reshape(BINS, qcount)
        radial_hi = radial.astype(jnp.bfloat16)
        radial_lo = (radial - radial_hi.astype(jnp.float32)).astype(jnp.bfloat16)
        there = slice(wide_at[j], wide_at[j] + wide)
        tops = [high[there, :BINS], high[there, BINS:]]
        lows = [low[there, :BINS], low[there, BINS:]]
        main = jnp.dot(
            jnp.concatenate(tops + lows, axis=0), radial_hi, preferred_element_type=jnp.float32
        )
        rest = jnp.dot(
            jnp.concatenate(tops, axis=0), radial_lo, preferred_element_type=jnp.float32
        )
        out = (main[: 2 * wide] + (main[2 * wide :] + rest))
        live = 2 * (place[0] + j) + 1
        order = lax.broadcasted_iota(jnp.int32, (wide, qcount), 0)
        mine = jnp.where(order < live, out[:wide], 0.0)
        other = jnp.where(order < live, out[wide:], 0.0)
        done = 0
        while done < thin[j]:
            part, row = divmod(thin_at[j] + done, height - 1)
            count = min(thin[j] - done, height - 1 - row)
            at = slice(part * height + row, part * height + row + count)
            keep[at, :] = mine[done : done + count]
            away[at, :] = other[done : done + count]
            done += count

    cuts = [(0, 5), (6, 13), (14, 21), (22, degs - 1)]
    for first, last in cuts:
        for copy in fetch[first : last + 1]:
            copy.wait()
        for j in range(first, last + 1):
            turn(j)
        bin_rows(first, last)
    wave_copy.wait()
    form_copy.wait()
    scaled = forms[...] * scale
    for j in range(degs):
        mix(j)
    for i in range(give.shape[0]):
        give[i] = coded(away[i * height : (i + 1) * height, :])


def local_amplitude(place, keys, harmonic, bessel, form, height, scale, rows, thin):
    degs, atoms, width = harmonic.shape
    qcount = form.shape[1]
    live_rows = sum(rows)
    outs = [
        jax.ShapeDtypeStruct((PLANE * height, qcount), jnp.float32),
        jax.ShapeDtypeStruct((PLANE, height, qcount), jnp.int16),
    ]
    return pl.pallas_call(
        functools.partial(amplitude_kernel, scale, rows, thin),
        in_specs=[
            pl.BlockSpec(memory_space=pltpu.SMEM),
            pl.BlockSpec(memory_space=pltpu.VMEM),
            pl.BlockSpec(memory_space=pl.ANY),
            pl.BlockSpec(memory_space=pl.ANY),
            pl.BlockSpec(memory_space=pl.ANY),
        ],
        out_specs=[pl.BlockSpec(memory_space=pltpu.VMEM)] * 2,
        out_shape=outs,
        scratch_shapes=[
            pltpu.VMEM((degs, atoms, width), jnp.bfloat16),
            pltpu.VMEM(bessel.shape, jnp.float32),
            pltpu.VMEM(form.shape, jnp.float32),
            pltpu.VMEM((atoms, 2 * BINS), jnp.bfloat16),
            pltpu.VMEM((live_rows, atoms), jnp.bfloat16),
            pltpu.VMEM((live_rows, 2 * BINS), jnp.bfloat16),
            pltpu.VMEM((live_rows, 2 * BINS), jnp.bfloat16),
            pltpu.VMEM(outs[0].shape, jnp.float32),
            pltpu.SemaphoreType.DMA((degs,)),
            pltpu.SemaphoreType.DMA,
            pltpu.SemaphoreType.DMA,
        ],
        compiler_params=pltpu.CompilerParams(vmem_limit_bytes=AMPLITUDE_MIB * 2**20),
        cost_estimate=pl.CostEstimate(
            flops=2 * live_rows * (2 * BINS * atoms + 6 * BINS * qcount),
            bytes_accessed=harmonic.size * 2 + bessel.size * 4,
            transcendentals=0,
        ),
    )(place, keys, harmonic, bessel, form)


def turn_kernel(rows, thin, place, mine, other, wigner, out, first, second):
    rots, degs, width, _ = wigner.shape
    qcount = mine.shape[2]

    height = mine.shape[1]

    def unpack(block, into):
        for i in range(block.shape[0]):
            at = i * (height - 1)
            into[at : at + height, :] = block[i].astype(jnp.float32)

    @pl.when(place[1] == 0)
    def _():
        unpack(mine, first)
        unpack(other, second)

    @pl.when(place[1] != 0)
    def _():
        unpack(other, first)
        unpack(mine, second)

    order = lax.broadcasted_iota(jnp.int32, (width, qcount), 0)
    acc = [jnp.zeros((8, qcount), jnp.float32)] * rots
    thin_at = starts(thin)
    for j in range(degs):
        wide, some, at = rows[j], thin[j], thin_at[j]
        right = jnp.where(order < some, second[at : at + width, :], 0.0).astype(jnp.bfloat16)
        blocks = jnp.concatenate([wigner[r, j][:wide] for r in range(rots)], axis=0)
        turned = jnp.dot(blocks, right, preferred_element_type=jnp.float32)
        left = jnp.where(order[:wide] < some, first[at : at + wide, :], 0.0)
        for r in range(rots):
            prod = turned[r * wide : (r + 1) * wide] * left
            acc[r] = acc[r] + jnp.sum(prod.reshape(wide // 8, 8, qcount), axis=0)
    for r in range(rots):
        out[r : r + 1, :] = jnp.sum(acc[r], axis=0, keepdims=True) * (0.5 / degs)


def local_intensity(place, mine, other, wigner, rows, thin):
    rots = wigner.shape[0]
    parts, height, qcount = mine.shape
    total = -(-(parts * (height - 1) + wigner.shape[2]) // 8) * 8
    vmem = pl.BlockSpec(memory_space=pltpu.VMEM)
    return pl.pallas_call(
        functools.partial(turn_kernel, rows, thin),
        in_specs=[pl.BlockSpec(memory_space=pltpu.SMEM), vmem, vmem, vmem],
        out_specs=vmem,
        out_shape=jax.ShapeDtypeStruct((rots, qcount), jnp.float32),
        scratch_shapes=[pltpu.VMEM((total, qcount), jnp.float32)] * 2,
        compiler_params=pltpu.CompilerParams(vmem_limit_bytes=TURN_MIB * 2**20),
        cost_estimate=pl.CostEstimate(
            flops=2 * wigner.size * qcount,
            bytes_accessed=wigner.size * 2 + mine.size * 4,
            transcendentals=0,
        ),
    )(place, mine, other, wigner)


def near_kernel(keep, recv, out):
    height = out.shape[1]
    for i in range(out.shape[0]):
        out[i] = coded(keep[i * height : (i + 1) * height, :] + decoded(recv[i]))


def plane_kernel(near, total, code):
    acc = decoded(near[0])
    for i in range(1, near.shape[0]):
        acc = acc + decoded(near[i])
    total[...] = acc
    code[...] = coded(acc)


def pair_kernel(part, recv, total, code):
    acc = part[...] + decoded(recv[...])
    total[...] = acc
    code[...] = coded(acc)


def whole_kernel(part, recv, out):
    block = (part[...] + decoded(recv[...])).astype(jnp.bfloat16)
    for i in range(out.shape[0]):
        out[i] = block


def whole_call(body, out_shape, limit, *args):
    spec = pl.BlockSpec(memory_space=pltpu.VMEM)
    return pl.pallas_call(
        body,
        in_specs=[spec] * len(args),
        out_specs=jax.tree.map(lambda _: spec, out_shape),
        out_shape=out_shape,
        compiler_params=pltpu.CompilerParams(vmem_limit_bytes=limit * 2**20),
    )(*args)


def per_device(harmonic, shell, atom_type, domain, form, bessel, wigner):
    atom_rows, local_deg, width = harmonic.shape
    qcount = form.shape[1]
    rows, thin = widths(local_deg, 16), widths(local_deg, 1)
    height = -(-sum(thin) // PLANE) + 1
    core = lax.axis_index("c")
    swap = [(0, 1), (1, 0)]
    place = jnp.stack([lax.axis_index("deg") * local_deg, core]).astype(jnp.int32)
    side = jnp.where(core == 0, domain, 1 - domain)
    keys = ((side * SHELLS + shell) * TYPES + atom_type)[None]
    keep, give = local_amplitude(
        place,
        keys,
        harmonic.transpose(1, 0, 2),
        bessel.transpose(1, 0, 2),
        form,
        height,
        (atom_rows * 128) ** -0.5,
        rows,
        thin,
    )
    recv = lax.ppermute(give, "c", swap)
    coded_shape = (height, qcount)
    near = whole_call(
        near_kernel,
        jax.ShapeDtypeStruct((PLANE,) + coded_shape, jnp.int16),
        LIMIT,
        keep,
        recv,
    )
    near = lax.all_to_all(near, NEAR, 0, 0)
    shapes = [
        jax.ShapeDtypeStruct((height, qcount), jnp.float32),
        jax.ShapeDtypeStruct(coded_shape, jnp.int16),
    ]
    part, code = whole_call(plane_kernel, shapes, LIMIT, near)
    code = lax.ppermute(code, FAR, [(0, 1), (1, 0), (2, 3), (3, 2)])
    part, code = whole_call(pair_kernel, shapes, LIMIT, part, code)
    code = lax.ppermute(code, FAR, [(1, 2), (2, 1), (3, 0), (0, 3)])
    spread = whole_call(
        whole_kernel,
        jax.ShapeDtypeStruct((PLANE, height, qcount), jnp.bfloat16),
        LIMIT,
        part,
        code,
    )
    mine = lax.all_to_all(spread, NEAR, 0, 0)
    other = lax.ppermute(mine, "c", swap)
    out = local_intensity(place, mine, other, wigner, rows, thin)
    return out + lax.ppermute(out, "deg", swap)


def solution(mesh):
    grid = Mesh(mesh.devices.reshape(4, 2, 4, 2, 2, 2), ("y", "xl", "zh", "zl", "c", "deg"))
    slab = ("y", "xl", "zh", "zl", "c")
    in_specs = (
        P(slab, "deg", None),
        P(slab),
        P(slab),
        P(slab),
        P(),
        P(None, "deg", None),
        P(slab, "deg", None, None),
    )
    return jax.shard_map(
        per_device, mesh=grid, in_specs=in_specs, out_specs=P(slab, None), check_vma=False
    )
```

```python
import functools
import jax
import jax.numpy as jnp
from jax import lax
from jax.experimental import pallas as pl
from jax.experimental.pallas import tpu as pltpu
from jax.sharding import Mesh, PartitionSpec as P

SHELLS = 64
TYPES = 8
BINS = SHELLS * TYPES
NEAR = ("y", "xl", "zl")
FAR = "zh"
PLANE = 16
LIMIT = 8
AMPLITUDE_MIB = 48
TURN_MIB = 16


def widths(local_deg, step):
    return [-(-(2 * (local_deg + j) + 1) // step) * step for j in range(local_deg)]


def starts(rows):
    return [sum(rows[:j]) for j in range(len(rows))]


def coded(x):
    last = x.shape[0] - 1
    order = lax.broadcasted_iota(jnp.int32, x.shape, 0)
    size = jnp.where(order < last, jnp.abs(x), 0.0)
    top = jnp.maximum(jnp.max(size, axis=0, keepdims=True), 1e-30)
    power = jnp.floor(jnp.log2(top)) + 1.0
    steps = jnp.clip(jnp.round(x * jnp.exp2(15.0 - power)), -32767.0, 32767.0)
    return jnp.where(order < last, steps, power).astype(jnp.int32).astype(jnp.int16)


def decoded(block):
    wide = block.astype(jnp.int32).astype(jnp.float32)
    return wide * jnp.exp2(wide[block.shape[0] - 1 :] - 15.0)


def amplitude_kernel(
    scale, rows, thin, place, keys, harmonic, bessel, form, keep, give,
    atoms, waves, forms, onehot, turned, high, low, away, atom_sems, wave_sem, form_sem,
):
    width = harmonic.shape[2]
    qcount = form.shape[1]
    degs = len(rows)
    fetch = [
        pltpu.make_async_copy(harmonic.at[j], atoms.at[j], atom_sems.at[j]) for j in range(degs)
    ]
    for copy in fetch:
        copy.start()
    wave_copy = pltpu.make_async_copy(bessel, waves, wave_sem)
    wave_copy.start()
    form_copy = pltpu.make_async_copy(form, forms, form_sem)
    form_copy.start()

    slots = lax.broadcasted_iota(jnp.int32, (width, 2 * BINS), 1).astype(jnp.float32)
    for i in range(atoms.shape[1] // width):
        line = keys[:, i * width : (i + 1) * width].astype(jnp.float32)
        tall = jnp.transpose(jnp.broadcast_to(line, (width, width)))
        same = slots == jnp.concatenate([tall] * (2 * BINS // width), axis=1)
        onehot[i * width : (i + 1) * width, :] = jnp.where(same, 1.0, 0.0).astype(jnp.bfloat16)
    height = give.shape[1]
    blank = jnp.zeros((8, qcount), jnp.float32)
    keep[keep.shape[0] - 8 :, :] = blank
    away[keep.shape[0] - 8 :, :] = blank

    wide_at, thin_at = starts(rows), starts(thin)

    def turn(j):
        turned[wide_at[j] : wide_at[j] + rows[j], :] = jnp.transpose(atoms[j])[: rows[j]]

    def bin_rows(first, last):
        there = slice(wide_at[first], wide_at[last] + rows[last])
        binned = jnp.dot(turned[there, :], onehot[...], preferred_element_type=jnp.float32)
        top = binned.astype(jnp.bfloat16)
        high[there, :] = top
        low[there, :] = (binned - top.astype(jnp.float32)).astype(jnp.bfloat16)

    def mix(j):
        wide = rows[j]
        radial = (waves[j][:, None, :] * scaled[None]).reshape(BINS, qcount)
        radial_hi = radial.astype(jnp.bfloat16)
        radial_lo = (radial - radial_hi.astype(jnp.float32)).astype(jnp.bfloat16)
        there = slice(wide_at[j], wide_at[j] + wide)
        tops = [high[there, :BINS], high[there, BINS:]]
        lows = [low[there, :BINS], low[there, BINS:]]
        main = jnp.dot(
            jnp.concatenate(tops + lows, axis=0), radial_hi, preferred_element_type=jnp.float32
        )
        rest = jnp.dot(
            jnp.concatenate(tops, axis=0), radial_lo, preferred_element_type=jnp.float32
        )
        out = (main[: 2 * wide] + (main[2 * wide :] + rest))
        live = 2 * (place[0] + j) + 1
        order = lax.broadcasted_iota(jnp.int32, (wide, qcount), 0)
        mine = jnp.where(order < live, out[:wide], 0.0)
        other = jnp.where(order < live, out[wide:], 0.0)
        done = 0
        while done < thin[j]:
            part, row = divmod(thin_at[j] + done, height - 1)
            count = min(thin[j] - done, height - 1 - row)
            at = slice(part * height + row, part * height + row + count)
            keep[at, :] = mine[done : done + count]
            away[at, :] = other[done : done + count]
            done += count

    cuts = [(0, 2), (3, 9), (10, 17), (18, degs - 1)]
    for first, last in cuts:
        for copy in fetch[first : last + 1]:
            copy.wait()
        for j in range(first, last + 1):
            turn(j)
        bin_rows(first, last)
    wave_copy.wait()
    form_copy.wait()
    scaled = forms[...] * scale
    for j in range(degs):
        mix(j)
    for i in range(give.shape[0]):
        give[i] = coded(away[i * height : (i + 1) * height, :])


def local_amplitude(place, keys, harmonic, bessel, form, height, scale, rows, thin):
    degs, atoms, width = harmonic.shape
    qcount = form.shape[1]
    live_rows = sum(rows)
    outs = [
        jax.ShapeDtypeStruct((PLANE * height, qcount), jnp.float32),
        jax.ShapeDtypeStruct((PLANE, height, qcount), jnp.int16),
    ]
    return pl.pallas_call(
        functools.partial(amplitude_kernel, scale, rows, thin),
        in_specs=[
            pl.BlockSpec(memory_space=pltpu.SMEM),
            pl.BlockSpec(memory_space=pltpu.VMEM),
            pl.BlockSpec(memory_space=pl.ANY),
            pl.BlockSpec(memory_space=pl.ANY),
            pl.BlockSpec(memory_space=pl.ANY),
        ],
        out_specs=[pl.BlockSpec(memory_space=pltpu.VMEM)] * 2,
        out_shape=outs,
        scratch_shapes=[
            pltpu.VMEM((degs, atoms, width), jnp.bfloat16),
            pltpu.VMEM(bessel.shape, jnp.float32),
            pltpu.VMEM(form.shape, jnp.float32),
            pltpu.VMEM((atoms, 2 * BINS), jnp.bfloat16),
            pltpu.VMEM((live_rows, atoms), jnp.bfloat16),
            pltpu.VMEM((live_rows, 2 * BINS), jnp.bfloat16),
            pltpu.VMEM((live_rows, 2 * BINS), jnp.bfloat16),
            pltpu.VMEM(outs[0].shape, jnp.float32),
            pltpu.SemaphoreType.DMA((degs,)),
            pltpu.SemaphoreType.DMA,
            pltpu.SemaphoreType.DMA,
        ],
        compiler_params=pltpu.CompilerParams(vmem_limit_bytes=AMPLITUDE_MIB * 2**20),
        cost_estimate=pl.CostEstimate(
            flops=2 * live_rows * (2 * BINS * atoms + 6 * BINS * qcount),
            bytes_accessed=harmonic.size * 2 + bessel.size * 4,
            transcendentals=0,
        ),
    )(place, keys, harmonic, bessel, form)


def turn_kernel(rows, thin, place, mine, other, wigner, out, first, second):
    rots, degs, width, _ = wigner.shape
    qcount = mine.shape[2]

    height = mine.shape[1]

    def unpack(block, into):
        for i in range(block.shape[0]):
            at = i * (height - 1)
            into[at : at + height, :] = block[i].astype(jnp.float32)

    @pl.when(place[1] == 0)
    def _():
        unpack(mine, first)
        unpack(other, second)

    @pl.when(place[1] != 0)
    def _():
        unpack(other, first)
        unpack(mine, second)

    order = lax.broadcasted_iota(jnp.int32, (width, qcount), 0)
    acc = [jnp.zeros((8, qcount), jnp.float32)] * rots
    thin_at = starts(thin)
    for j in range(degs):
        wide, some, at = rows[j], thin[j], thin_at[j]
        right = jnp.where(order < some, second[at : at + width, :], 0.0).astype(jnp.bfloat16)
        blocks = jnp.concatenate([wigner[r, j][:wide] for r in range(rots)], axis=0)
        turned = jnp.dot(blocks, right, preferred_element_type=jnp.float32)
        left = jnp.where(order[:wide] < some, first[at : at + wide, :], 0.0)
        for r in range(rots):
            prod = turned[r * wide : (r + 1) * wide] * left
            acc[r] = acc[r] + jnp.sum(prod.reshape(wide // 8, 8, qcount), axis=0)
    for r in range(rots):
        out[r : r + 1, :] = jnp.sum(acc[r], axis=0, keepdims=True) * (0.5 / degs)


def local_intensity(place, mine, other, wigner, rows, thin):
    rots = wigner.shape[0]
    parts, height, qcount = mine.shape
    total = -(-(parts * (height - 1) + wigner.shape[2]) // 8) * 8
    vmem = pl.BlockSpec(memory_space=pltpu.VMEM)
    return pl.pallas_call(
        functools.partial(turn_kernel, rows, thin),
        in_specs=[pl.BlockSpec(memory_space=pltpu.SMEM), vmem, vmem, vmem],
        out_specs=vmem,
        out_shape=jax.ShapeDtypeStruct((rots, qcount), jnp.float32),
        scratch_shapes=[pltpu.VMEM((total, qcount), jnp.float32)] * 2,
        compiler_params=pltpu.CompilerParams(vmem_limit_bytes=TURN_MIB * 2**20),
        cost_estimate=pl.CostEstimate(
            flops=2 * wigner.size * qcount,
            bytes_accessed=wigner.size * 2 + mine.size * 4,
            transcendentals=0,
        ),
    )(place, mine, other, wigner)


def near_kernel(keep, recv, out):
    height = out.shape[1]
    for i in range(out.shape[0]):
        out[i] = coded(keep[i * height : (i + 1) * height, :] + decoded(recv[i]))


def plane_kernel(near, total, code):
    acc = decoded(near[0])
    for i in range(1, near.shape[0]):
        acc = acc + decoded(near[i])
    total[...] = acc
    code[...] = coded(acc)


def pair_kernel(part, recv, total, code):
    acc = part[...] + decoded(recv[...])
    total[...] = acc
    code[...] = coded(acc)


def whole_kernel(part, recv, out):
    block = (part[...] + decoded(recv[...])).astype(jnp.bfloat16)
    for i in range(out.shape[0]):
        out[i] = block


def whole_call(body, out_shape, limit, *args):
    spec = pl.BlockSpec(memory_space=pltpu.VMEM)
    return pl.pallas_call(
        body,
        in_specs=[spec] * len(args),
        out_specs=jax.tree.map(lambda _: spec, out_shape),
        out_shape=out_shape,
        compiler_params=pltpu.CompilerParams(vmem_limit_bytes=limit * 2**20),
    )(*args)


def per_device(harmonic, shell, atom_type, domain, form, bessel, wigner):
    atom_rows, local_deg, width = harmonic.shape
    qcount = form.shape[1]
    rows, thin = widths(local_deg, 16), widths(local_deg, 1)
    height = -(-sum(thin) // PLANE) + 1
    core = lax.axis_index("c")
    swap = [(0, 1), (1, 0)]
    place = jnp.stack([lax.axis_index("deg") * local_deg, core]).astype(jnp.int32)
    side = jnp.where(core == 0, domain, 1 - domain)
    keys = ((side * SHELLS + shell) * TYPES + atom_type)[None]
    keep, give = local_amplitude(
        place,
        keys,
        harmonic.transpose(1, 0, 2),
        bessel.transpose(1, 0, 2),
        form,
        height,
        (atom_rows * 128) ** -0.5,
        rows,
        thin,
    )
    recv = lax.ppermute(give, "c", swap)
    coded_shape = (height, qcount)
    near = whole_call(
        near_kernel,
        jax.ShapeDtypeStruct((PLANE,) + coded_shape, jnp.int16),
        LIMIT,
        keep,
        recv,
    )
    near = lax.all_to_all(near, NEAR, 0, 0)
    shapes = [
        jax.ShapeDtypeStruct((height, qcount), jnp.float32),
        jax.ShapeDtypeStruct(coded_shape, jnp.int16),
    ]
    part, code = whole_call(plane_kernel, shapes, LIMIT, near)
    code = lax.ppermute(code, FAR, [(0, 1), (1, 0), (2, 3), (3, 2)])
    part, code = whole_call(pair_kernel, shapes, LIMIT, part, code)
    code = lax.ppermute(code, FAR, [(1, 2), (2, 1), (3, 0), (0, 3)])
    spread = whole_call(
        whole_kernel,
        jax.ShapeDtypeStruct((PLANE, height, qcount), jnp.bfloat16),
        LIMIT,
        part,
        code,
    )
    mine = lax.all_to_all(spread, NEAR, 0, 0)
    other = lax.ppermute(mine, "c", swap)
    out = local_intensity(place, mine, other, wigner, rows, thin)
    return out + lax.ppermute(out, "deg", swap)


def solution(mesh):
    grid = Mesh(mesh.devices.reshape(4, 2, 4, 2, 2, 2), ("y", "xl", "zh", "zl", "c", "deg"))
    slab = ("y", "xl", "zh", "zl", "c")
    in_specs = (
        P(slab, "deg", None),
        P(slab),
        P(slab),
        P(slab),
        P(),
        P(None, "deg", None),
        P(slab, "deg", None, None),
    )
    return jax.shard_map(
        per_device, mesh=grid, in_specs=in_specs, out_specs=P(slab, None), check_vma=False
    )
```
